32 devices in a mesh: dp: 16 (over z, y, x), mp: 2 (over core).
Axes of the slice: x: 2, y: 2, z: 4, core: 2. Of those that a mesh axis runs over, the one named last changes fastest.
Arguments:
- activations: bfloat16 [4096, 4096], P('dp', 'mp'), may hold values from -6 to 6
- out_grad: bfloat16 [4096, 14336], P('dp', 'mp'), may hold values from -6 to 6
- row_blocks: int32 [112, 8], P('mp'), may hold values from 0 to 31, as said below
- doc_lengths: int32 [16, 4], P('dp'), may hold values from 0 to 256, as said below
Outputs:
- weight_grad: float32 [112, 1024, 128], P('mp', 'dp')
The draws below stay inside these ranges and needn't reach their ends.
Inputs may be any that keep to these rules, and one draw needn't show every extreme that they name: `row_blocks`: each row holds 8 distinct row-block indices. `doc_lengths`: the lengths of one index of dp sum to at most 256; at some index one document fills all 256 slots.
All inputs are finite; a program needn't handle non-finite values.
Results may differ from the reference program's by a relative error of at most 0.0003.
Values may be sent and summed in bfloat16 or wider, within the bound.
No kernel may reach another device: no remote copies, remote signals or barrier semaphores. Data moves between devices by JAX's collectives and lax.ppermute only.
A program may use at most 128 MiB of HBM per device.

```python
import jax
import jax.numpy as jnp
from jax import lax

D = 4096
FF = 14336
BLOCK = 128
TOK_DEV = 256
DOCS = 4
RB = 32
NCB = 112
KNZ = 8
TOKENS = 4096
N_DP = 16


def draw_row_blocks(key, part):
    key = jax.random.fold_in(key, 11)
    keys = jax.random.split(key, NCB)
    picks = jax.vmap(lambda one: jax.random.permutation(one, RB)[:KNZ])(keys)
    return picks.astype(jnp.int32)


def draw_doc_lengths(key, part):
    key = jax.random.fold_in(key, 23)
    key_shift, key_cut, key_full, key_split = jax.random.split(key, 4)
    shift = jax.random.randint(key_shift, (N_DP,), 0, 3)
    base = jnp.int32(TOK_DEV) // jnp.left_shift(jnp.int32(1), shift.astype(jnp.int32))
    cut = jax.random.randint(key_cut, (N_DP,), 0, base // 4 + 1)
    totals = base - cut
    full = jax.random.randint(key_full, (), 0, N_DP)
    is_full = jnp.arange(N_DP) == full
    totals = jnp.where(is_full, jnp.int32(TOK_DEV), totals).astype(jnp.int32)
    cuts = jax.random.randint(key_split, (N_DP, DOCS - 1), 0, totals[:, None] + 1)
    cuts = jnp.where(is_full[:, None], jnp.int32(0), cuts).astype(jnp.int32)
    cuts = jnp.sort(cuts, axis=1)
    edges = jnp.concatenate([jnp.zeros((N_DP, 1), jnp.int32), cuts.astype(jnp.int32), totals[:, None]], axis=1)
    return (edges[:, 1:] - edges[:, :-1]).astype(jnp.int32)


def steps_of(own_key, shape, cuts, smallest, largest):
    factor_of, own = 1.0, jax.random.fold_in(own_key, 6)
    for axis_at, parts in cuts:
        draws = jnp.exp(jax.random.uniform(jax.random.fold_in(own, axis_at), (parts,), jnp.float32, smallest / len(cuts), largest / len(cuts)))
        factor_of = factor_of * jnp.repeat(draws, shape[axis_at] // parts).reshape([-1 if axis == axis_at else 1 for axis in range(len(shape))])
    return factor_of


def normal_values(own_key, shape, scale, bound, cuts=(), held_as=jnp.bfloat16):
    entries = jax.random.normal(own_key, shape, jnp.float32) * scale
    if len(cuts) > 0:
        entries = steps_of(own_key, shape, cuts, -0.22, 0.18) * entries
    return jnp.clip(entries, min=-bound, max=bound).astype(held_as)


def setup_inputs(seed: int = 0) -> dict:
    seeds = jax.random.split(jax.random.key(seed), 5)
    activations = normal_values(seeds[0], (TOKENS, D), 1.0, 6.0, ((0, 16), (1, 2)))
    out_grad = normal_values(seeds[1], (TOKENS, FF), 1.0, 6.0, ((0, 16), (1, 2)))
    row_blocks = draw_row_blocks(jax.random.fold_in(seeds[4], 71), 0)
    doc_lengths = draw_doc_lengths(jax.random.fold_in(seeds[4], 71), 0)
    return {"activations": activations, "out_grad": out_grad, "row_blocks": row_blocks, "doc_lengths": doc_lengths}


def reference(activations, out_grad, row_blocks, doc_lengths):
    live = lax.optimization_barrier(jnp.sum(doc_lengths, axis=1))
    slots = jnp.arange(TOK_DEV, dtype=jnp.int32)
    keep = (slots[None, :] < live[:, None]).reshape(-1)
    masked = jnp.where(keep[:, None], out_grad, jnp.zeros_like(out_grad))
    blocked = activations.reshape(activations.shape[0], RB, BLOCK)
    factor = jnp.float32(1.0) / jnp.sqrt(jnp.float32(TOKENS))

    def one_column(column):
        chosen = jnp.take(blocked, row_blocks[column], axis=1).reshape(activations.shape[0], KNZ * BLOCK)
        grads = lax.dynamic_slice_in_dim(masked, column * BLOCK, BLOCK, 1)
        total = lax.dot_general(chosen, grads, (((0,), (0,)), ((), ())), preferred_element_type=jnp.float32)
        return total * factor
    return lax.map(one_column, jnp.arange(NCB, dtype=jnp.int32))
```

```python
import functools

import jax
import jax.numpy as jnp
from jax import lax
from jax.experimental import pallas as pl
from jax.experimental.pallas import tpu as pltpu
from jax.sharding import PartitionSpec as P

BLOCK = 128
LEVELS = 32700.0
STEPS = 128.0
SMALLEST = 2.0**-110
VMEM_LIMIT = 16 * 1024 * 1024


def pad16(rows):
    return -(-rows // 16) * 16


def params():
    return pltpu.CompilerParams(vmem_limit_bytes=VMEM_LIMIT)


def encode(values):
    largest = jnp.max(jnp.abs(values), axis=0, keepdims=True)
    power = jnp.ceil(jnp.log2(jnp.maximum(largest, SMALLEST)) * STEPS)
    codes = jnp.round(values * (jnp.exp2(power * (-1.0 / STEPS)) * LEVELS))
    return codes.astype(jnp.int32).astype(jnp.int16), power


def send_powers(sent, powers, body):
    sent[pl.ds(body, powers.shape[0]), :] = powers[...].astype(jnp.int32).astype(jnp.int16)


def read_scales(got, scales, body):
    coded = got[pl.ds(body, scales.shape[0]), :].astype(jnp.int32).astype(jnp.float32)
    scales[...] = jnp.exp2(coded * (1.0 / STEPS)) * (1.0 / LEVELS)


def multiply_kernel(width, rows, height, order, me, picks, turned, own_g, near_g, _, keep, sent, powers):
    half = len(order) // 2
    slots = own_g.shape[0]
    per_block = height // rows

    def column(c, _):
        lanes = pl.ds(pl.multiple_of(c * BLOCK, BLOCK), BLOCK)

        def product(masks):
            starts = []
            for mask in masks:
                piece = me[0] ^ mask
                entry, part = piece // per_block, piece % per_block
                starts.append(pl.multiple_of(picks[c, entry] * height + part * rows, rows))
            left = jnp.concatenate([turned[pl.ds(s, rows), :] for s in starts], axis=0)
            return jnp.dot(left[:, :slots], own_g[:, lanes], preferred_element_type=jnp.float32) + jnp.dot(
                left[:, slots:], near_g[:, lanes], preferred_element_type=jnp.float32
            )

        at = pl.ds(pl.multiple_of(c * (half * rows), half * rows), half * rows)
        away = product(order[half:])
        for j in range(half):
            codes, power = encode(away[j * rows : (j + 1) * rows])
            sent[pl.ds(pl.multiple_of((c * half + j) * rows, rows), rows), :] = codes
            powers[pl.ds(c * half + j, 1), :] = power
        keep[at, :] = product(order[:half])
        return 0

    lax.fori_loop(0, width, column, 0)
    send_powers(sent, powers, width * half * rows)


def combine_kernel(width, rows, pieces, factor, keep, got, _, *rest):
    if pieces > 1:
        mine, sent, scales, powers = rest
    else:
        mine, scales = rest
    half = pieces // 2
    read_scales(got, scales, width * pieces * rows)

    def column(c, _):
        def summed(j):
            at = pl.ds(pl.multiple_of((c * pieces + j) * rows, rows), rows)
            return keep[at, :] + got[at, :].astype(jnp.int32).astype(jnp.float32) * scales[pl.ds(c * pieces + j, 1), :]

        for j in range(half):
            to = pl.ds(pl.multiple_of((c * half + j) * rows, rows), rows)
            codes, power = encode(summed(half + j))
            sent[to, :] = codes
            powers[pl.ds(c * half + j, 1), :] = power
            mine[to, :] = summed(j)
        if pieces == 1:
            mine[c] = summed(0) * factor
        return 0

    lax.fori_loop(0, width, column, 0)
    if pieces > 1:
        send_powers(sent, powers, width * half * rows)


def widths_of(columns):
    if columns <= 12:
        return [columns]
    middle = columns - 8
    parts = -(-middle // 8)
    cuts = [middle * i // parts for i in range(parts + 1)]
    return [4] + [b - a for a, b in zip(cuts, cuts[1:])] + [4]


def masks_of(bits):
    masks = [0]
    for bit in reversed(bits):
        masks = masks + [m | 1 << bit for m in masks]
    return masks


def shards(owners, groups, activations, out_grad, row_blocks, doc_lengths):
    slots, features = activations.shape
    columns, entries = row_blocks.shape
    rows = entries * BLOCK // owners
    per_block = BLOCK // rows
    height = BLOCK // 2
    factor = 1.0 / float(slots * owners) ** 0.5
    pieces = owners // 2
    bits = list(range(pieces.bit_length() - 1))
    widths = widths_of(columns)
    count = len(widths)
    starts = [sum(widths[:i]) for i in range(count)]

    me = lax.axis_index("dp")
    half, place = me % 2, (me // 2).astype(jnp.int32).reshape(1)
    beside = [(i, i ^ 1) for i in range(owners)]

    def cut(i):
        return out_grad[:, starts[i] * BLOCK : (starts[i] + widths[i]) * BLOCK]

    def fetch(piece, after):
        piece, after = lax.optimization_barrier((piece, after))
        return lax.ppermute(piece, "dp", beside), after

    own_g = [cut(i) for i in range(count)]
    near_g = {0: lax.ppermute(own_g[0], "dp", beside)}

    live = jnp.sum(doc_lengths)
    keep = jnp.arange(slots, dtype=jnp.int32) < live
    masked = jnp.where(keep[:, None], activations, jnp.zeros_like(activations))
    split = masked.T.reshape(features // BLOCK, per_block // 2, 2, rows, slots)
    halves = [
        lax.dynamic_index_in_dim(split, h, 2, keepdims=False).reshape(features // 2, slots) for h in (half, 1 - half)
    ]
    near_half = lax.ppermute(halves[1], "dp", beside)
    near_half, near_g[0] = lax.optimization_barrier((near_half, near_g[0]))
    if count > 1:
        near_g[1], halves[0] = fetch(own_g[1], halves[0])

    def spread(part):
        return [part] + [
            lax.ppermute(part, "mp", [(g, (g + s) % groups) for g in range(groups)]) for s in range(1, groups)
        ]

    own_t, near_t = spread(halves[0]), spread(near_half)
    turned = jnp.concatenate([jnp.concatenate(own_t, axis=0), jnp.concatenate(near_t, axis=0)], axis=1)
    blocks = features // BLOCK
    picks = (lax.axis_index("mp") - row_blocks // blocks) % groups * blocks + row_blocks % blocks

    vmem = pl.BlockSpec(memory_space=pltpu.VMEM)
    smem = pl.BlockSpec(memory_space=pltpu.SMEM)

    def coded(width, n):
        return jax.ShapeDtypeStruct((width * n * rows + pad16(width * n), BLOCK), jnp.int16)

    def sums(width, n):
        return jax.ShapeDtypeStruct((width * n * rows, BLOCK), jnp.float32)

    def scale(width, n):
        return pltpu.VMEM((pad16(width * n), BLOCK), jnp.float32)

    small = pl.CostEstimate(flops=1024, bytes_accessed=1024, transcendentals=0)
    anywhere = pl.BlockSpec(memory_space=pl.ANY)

    def multiply(i, order, last):
        width, n = widths[i], pieces // 2
        chosen = picks[starts[i] : starts[i] + width]
        return pl.pallas_call(
            functools.partial(multiply_kernel, width, rows, height, order),
            out_shape=[sums(width, n), coded(width, n)],
            in_specs=[smem, smem, vmem, vmem, vmem, anywhere],
            out_specs=[vmem, vmem],
            scratch_shapes=[scale(width, n)],
            compiler_params=params(),
            cost_estimate=small,
            name="multiply",
        )(place, chosen, turned, own_g[i], near_g[i], last)

    def combine(i, n, kept, got, last):
        width = widths[i]
        if n > 1:
            outs = [sums(width, n // 2), coded(width, n // 2)]
            scratch = [scale(width, n), scale(width, n // 2)]
        else:
            outs = [jax.ShapeDtypeStruct((width, rows, BLOCK), jnp.float32)]
            scratch = [scale(width, n)]
        return pl.pallas_call(
            functools.partial(combine_kernel, width, rows, n, factor),
            out_shape=outs,
            in_specs=[vmem, vmem, anywhere],
            out_specs=[vmem] * len(outs),
            scratch_shapes=scratch,
            compiler_params=params(),
            cost_estimate=small,
            name="combine",
        )(kept, got, last)

    def swap(sent, bit):
        return lax.ppermute(sent, "dp", [(o, o ^ (2 << bit)) for o in range(owners)])

    depth = len(bits)
    held, outputs, last = {}, [None] * count, place
    for tick in range(count + depth):
        if tick < count:
            kept, sent = multiply(tick, masks_of(bits), last)
            last = kept
            if tick + 2 < count:
                near_g[tick + 2], kept = fetch(own_g[tick + 2], kept)
            held[tick] = (pieces // 2, kept, swap(sent, bits[0]))
        for step in range(1, depth + 1):
            i = tick - step
            if 0 <= i < count:
                n, kept, got = held[i]
                result = combine(i, n, kept, got, last)
                last = result[0]
                if n > 1:
                    held[i] = (n // 2, result[0], swap(result[1], bits[step]))
                else:
                    outputs[i] = result[0]
    return jnp.concatenate(outputs, axis=0)


def solution(mesh):
    in_specs = (P("dp", "mp"), P("dp", "mp"), P("mp", None), P("dp", None))
    out_specs = P("mp", "dp", None)
    body = functools.partial(shards, mesh.shape["dp"], mesh.shape["mp"])
    return jax.shard_map(body, mesh=mesh, in_specs=in_specs, out_specs=out_specs, check_vma=False)
```

```python
import functools

import jax
import jax.numpy as jnp
from jax import lax
from jax.experimental import pallas as pl
from jax.experimental.pallas import tpu as pltpu
from jax.sharding import PartitionSpec as P

BLOCK = 128
LEVELS = 32700.0
STEPS = 128.0
SMALLEST = 2.0**-110
VMEM_LIMIT = 16 * 1024 * 1024


def pad16(rows):
    return -(-rows // 16) * 16


def params():
    return pltpu.CompilerParams(vmem_limit_bytes=VMEM_LIMIT)


def encode(values):
    largest = jnp.max(jnp.abs(values), axis=0, keepdims=True)
    power = jnp.ceil(jnp.log2(jnp.maximum(largest, SMALLEST)) * STEPS)
    codes = jnp.round(values * (jnp.exp2(power * (-1.0 / STEPS)) * LEVELS))
    return codes.astype(jnp.int32).astype(jnp.int16), power


def send_powers(sent, powers, body):
    sent[pl.ds(body, powers.shape[0]), :] = powers[...].astype(jnp.int32).astype(jnp.int16)


def read_scales(got, scales, body):
    coded = got[pl.ds(body, scales.shape[0]), :].astype(jnp.int32).astype(jnp.float32)
    scales[...] = jnp.exp2(coded * (1.0 / STEPS)) * (1.0 / LEVELS)


def multiply_kernel(width, rows, height, order, me, picks, turned, own_g, near_g, _, keep, sent, powers):
    half = len(order) // 2
    slots = own_g.shape[0]
    per_block = height // rows

    def column(c, _):
        lanes = pl.ds(pl.multiple_of(c * BLOCK, BLOCK), BLOCK)

        def product(masks):
            starts = []
            for mask in masks:
                piece = me[0] ^ mask
                entry, part = piece // per_block, piece % per_block
                starts.append(pl.multiple_of(picks[c, entry] * height + part * rows, rows))
            left = jnp.concatenate([turned[pl.ds(s, rows), :] for s in starts], axis=0)
            return jnp.dot(left[:, :slots], own_g[:, lanes], preferred_element_type=jnp.float32) + jnp.dot(
                left[:, slots:], near_g[1 - me[1], :, lanes], preferred_element_type=jnp.float32
            )

        at = pl.ds(pl.multiple_of(c * (half * rows), half * rows), half * rows)
        away = product(order[half:])
        for j in range(half):
            codes, power = encode(away[j * rows : (j + 1) * rows])
            sent[pl.ds(pl.multiple_of((c * half + j) * rows, rows), rows), :] = codes
            powers[pl.ds(c * half + j, 1), :] = power
        keep[at, :] = product(order[:half])
        return 0

    lax.fori_loop(0, width, column, 0)
    send_powers(sent, powers, width * half * rows)


def combine_kernel(width, rows, pieces, factor, keep, got, _, *rest):
    if pieces > 1:
        mine, sent, scales, powers = rest
    else:
        mine, scales = rest
    half = pieces // 2
    read_scales(got, scales, width * pieces * rows)

    def column(c, _):
        def summed(j):
            at = pl.ds(pl.multiple_of((c * pieces + j) * rows, rows), rows)
            return keep[at, :] + got[at, :].astype(jnp.int32).astype(jnp.float32) * scales[pl.ds(c * pieces + j, 1), :]

        for j in range(half):
            to = pl.ds(pl.multiple_of((c * half + j) * rows, rows), rows)
            codes, power = encode(summed(half + j))
            sent[to, :] = codes
            powers[pl.ds(c * half + j, 1), :] = power
            mine[to, :] = summed(j)
        if pieces == 1:
            mine[c] = summed(0) * factor
        return 0

    lax.fori_loop(0, width, column, 0)
    if pieces > 1:
        send_powers(sent, powers, width * half * rows)


def widths_of(columns):
    if columns <= 12:
        return [columns]
    middle = columns - 8
    parts = -(-middle // 8)
    cuts = [middle * i // parts for i in range(parts + 1)]
    return [4] + [b - a for a, b in zip(cuts, cuts[1:])] + [4]


def masks_of(bits):
    masks = [0]
    for bit in reversed(bits):
        masks = masks + [m | 1 << bit for m in masks]
    return masks


def shards(owners, groups, activations, out_grad, row_blocks, doc_lengths):
    slots, features = activations.shape
    columns, entries = row_blocks.shape
    rows = entries * BLOCK // owners
    per_block = BLOCK // rows
    height = BLOCK // 2
    factor = 1.0 / float(slots * owners) ** 0.5
    pieces = owners // 2
    bits = list(range(pieces.bit_length() - 1))
    widths = widths_of(columns)
    count = len(widths)
    starts = [sum(widths[:i]) for i in range(count)]

    me = lax.axis_index("dp")
    half, place = me % 2, jnp.stack([me // 2, me % 2]).astype(jnp.int32)
    beside = [(i, i ^ 1) for i in range(owners)]

    def cut(i):
        return out_grad[:, starts[i] * BLOCK : (starts[i] + widths[i]) * BLOCK]

    def fetch(piece, after):
        piece, after = lax.optimization_barrier((piece, after))
        return both(piece), after

    pairs = [[i, i + 1] for i in range(0, owners, 2)]

    def both(piece):
        return lax.all_gather(piece, "dp", axis_index_groups=pairs)

    own_g = [cut(i) for i in range(count)]
    near_g = {0: both(own_g[0])}

    live = jnp.sum(doc_lengths)
    keep = jnp.arange(slots, dtype=jnp.int32) < live
    masked = jnp.where(keep[:, None], activations, jnp.zeros_like(activations))
    split = masked.T.reshape(features // BLOCK, per_block // 2, 2, rows, slots)
    halves = [
        lax.dynamic_index_in_dim(split, h, 2, keepdims=False).reshape(features // 2, slots) for h in (half, 1 - half)
    ]
    near_half = lax.ppermute(halves[1], "dp", beside)
    near_half, near_g[0] = lax.optimization_barrier((near_half, near_g[0]))
    if count > 1:
        near_g[1], halves[0] = fetch(own_g[1], halves[0])

    def spread(part):
        return [part] + [
            lax.ppermute(part, "mp", [(g, (g + s) % groups) for g in range(groups)]) for s in range(1, groups)
        ]

    own_t, near_t = spread(halves[0]), spread(near_half)
    turned = jnp.concatenate([jnp.concatenate(own_t, axis=0), jnp.concatenate(near_t, axis=0)], axis=1)
    blocks = features // BLOCK
    picks = (lax.axis_index("mp") - row_blocks // blocks) % groups * blocks + row_blocks % blocks

    vmem = pl.BlockSpec(memory_space=pltpu.VMEM)
    smem = pl.BlockSpec(memory_space=pltpu.SMEM)

    def coded(width, n):
        return jax.ShapeDtypeStruct((width * n * rows + pad16(width * n), BLOCK), jnp.int16)

    def sums(width, n):
        return jax.ShapeDtypeStruct((width * n * rows, BLOCK), jnp.float32)

    def scale(width, n):
        return pltpu.VMEM((pad16(width * n), BLOCK), jnp.float32)

    small = pl.CostEstimate(flops=1024, bytes_accessed=1024, transcendentals=0)
    anywhere = pl.BlockSpec(memory_space=pl.ANY)

    def multiply(i, order, last):
        width, n = widths[i], pieces // 2
        chosen = picks[starts[i] : starts[i] + width]
        return pl.pallas_call(
            functools.partial(multiply_kernel, width, rows, height, order),
            out_shape=[sums(width, n), coded(width, n)],
            in_specs=[smem, smem, vmem, vmem, vmem, anywhere],
            out_specs=[vmem, vmem],
            scratch_shapes=[scale(width, n)],
            compiler_params=params(),
            cost_estimate=small,
            name="multiply",
        )(place, chosen, turned, own_g[i], near_g[i], last)

    def combine(i, n, kept, got, last):
        width = widths[i]
        if n > 1:
            outs = [sums(width, n // 2), coded(width, n // 2)]
            scratch = [scale(width, n), scale(width, n // 2)]
        else:
            outs = [jax.ShapeDtypeStruct((width, rows, BLOCK), jnp.float32)]
            scratch = [scale(width, n)]
        return pl.pallas_call(
            functools.partial(combine_kernel, width, rows, n, factor),
            out_shape=outs,
            in_specs=[vmem, vmem, anywhere],
            out_specs=[vmem] * len(outs),
            scratch_shapes=scratch,
            compiler_params=params(),
            cost_estimate=small,
            name="combine",
        )(kept, got, last)

    def swap(sent, bit):
        return lax.ppermute(sent, "dp", [(o, o ^ (2 << bit)) for o in range(owners)])

    depth = len(bits)
    held, outputs, last = {}, [None] * count, place
    for tick in range(count + depth):
        if tick < count:
            kept, sent = multiply(tick, masks_of(bits), last)
            last = kept
            if tick + 2 < count:
                near_g[tick + 2], kept = fetch(own_g[tick + 2], kept)
            held[tick] = (pieces // 2, kept, swap(sent, bits[0]))
        for step in range(1, depth + 1):
            i = tick - step
            if 0 <= i < count:
                n, kept, got = held[i]
                result = combine(i, n, kept, got, last)
                last = result[0]
                if n > 1:
                    held[i] = (n // 2, result[0], swap(result[1], bits[step]))
                else:
                    outputs[i] = result[0]
    return jnp.concatenate(outputs, axis=0)


def solution(mesh):
    in_specs = (P("dp", "mp"), P("dp", "mp"), P("mp", None), P("dp", None))
    out_specs = P("mp", "dp", None)
    body = functools.partial(shards, mesh.shape["dp"], mesh.shape["mp"])
    return jax.shard_map(body, mesh=mesh, in_specs=in_specs, out_specs=out_specs, check_vma=False)
```

```python
import functools

import jax
import jax.numpy as jnp
from jax import lax
from jax.experimental import pallas as pl
from jax.experimental.pallas import tpu as pltpu
from jax.sharding import PartitionSpec as P

BLOCK = 128
LEVELS = 32700.0
STEPS = 128.0
SMALLEST = 2.0**-110
PAD = 16
VMEM_LIMIT = 16 * 1024 * 1024


def pad16(rows):
    return -(-rows // 16) * 16


def params():
    return pltpu.CompilerParams(vmem_limit_bytes=VMEM_LIMIT)


def encode(values):
    largest = jnp.max(jnp.abs(values), axis=0, keepdims=True)
    power = jnp.ceil(jnp.log2(jnp.maximum(largest, SMALLEST)) * STEPS)
    codes = jnp.round(values * (jnp.exp2(power * (-1.0 / STEPS)) * LEVELS))
    return codes.astype(jnp.int32).astype(jnp.int16), power


def send_powers(sent, powers, body):
    sent[pl.ds(body, powers.shape[0]), :] = powers[...].astype(jnp.int32).astype(jnp.int16)


def read_scales(got, scales, body):
    coded = got[pl.ds(body, scales.shape[0]), :].astype(jnp.int32).astype(jnp.float32)
    scales[...] = jnp.exp2(coded * (1.0 / STEPS)) * (1.0 / LEVELS)


def each(width, column):
    at_once = max(n for n in (1, 2, 3) if width % n == 0)

    def step(i, _):
        for j in range(at_once):
            column(i * at_once + j)
        return 0

    lax.fori_loop(0, width // at_once, step, 0)


def prepare_kernel(rows, me, lengths, activations, own, other):
    slots, features = activations.shape
    live = lengths[0, 0]
    for i in range(1, lengths.shape[1]):
        live = live + lengths[0, i]
    keep = lax.broadcasted_iota(jnp.int32, (BLOCK, slots), 1) < live
    for b in range(features // BLOCK):
        block = activations[:, b * BLOCK : (b + 1) * BLOCK].astype(jnp.float32).T
        block = jnp.where(keep, block, 0.0).astype(activations.dtype)
        for p in range(BLOCK // rows):
            to = pl.ds((b * (BLOCK // rows) + p) // 2 * rows, rows)
            piece = block[p * rows : (p + 1) * rows]

            @pl.when(me[0] % 2 == p % 2)
            def _():
                own[to, :] = piece

            @pl.when(me[0] % 2 != p % 2)
            def _():
                other[to, :] = piece


def multiply_kernel(width, rows, height, order, pairs, begins, me, picks, *refs):
    lefts, grads = refs[: len(pairs)], refs[len(pairs) : -4]
    keep, sent, powers = refs[-3:]
    half = len(order) // 2
    per_block = height // rows
    slots = lefts[0].shape[1]

    def column(c):
        lanes = [pl.ds(pl.multiple_of((begin + c) * BLOCK, BLOCK), BLOCK) for begin in begins]

        def product(masks):
            starts = []
            for mask in masks:
                piece = (me[0] ^ mask) // 2
                entry, part = piece // per_block, piece % per_block
                starts.append((mask & 1, pl.multiple_of(picks[c, entry] * height + part * rows, rows)))
            total = None
            for t, grad in enumerate(grads):
                left = [lefts[pairs.index((x, t))][pl.ds(s, rows), :] for x, s in starts]
                term = jnp.dot(
                    jnp.concatenate(left, axis=0), grad[:slots, lanes[t]], preferred_element_type=jnp.float32
                )
                total = term if total is None else total + term
            return total

        away = product(order[half:])
        for j in range(half):
            codes, power = encode(away[j * rows : (j + 1) * rows])
            sent[pl.ds(pl.multiple_of((c * half + j) * rows, rows), rows), :] = codes
            powers[pl.ds(c * half + j, 1), :] = power
        keep[pl.ds(pl.multiple_of(c * (half * rows), half * rows), half * rows), :] = product(order[:half])

    each(width, column)
    send_powers(sent, powers, width * half * rows)


def combine_kernel(sources, rows, pieces, coded, factor, *refs):
    count = sum(1 + has for _, has in sources)
    inputs, refs = list(refs[:count]), refs[count + 1 :]
    half = pieces // 2
    outs = 2 if coded else 1
    out, scales = refs[0], list(refs[outs:])
    if coded:
        sent, powers = refs[1], scales.pop()
    begin = 0
    for width, has in sources:
        keep = inputs.pop(0)
        got, scale = (inputs.pop(0), scales.pop(0)) if has else (None, None)
        if has:
            read_scales(got, scale, width * pieces * rows)

        def column(c, keep=keep, got=got, scale=scale, begin=begin):
            def summed(j):
                at = pl.ds(pl.multiple_of((c * pieces + j) * rows, rows), rows)
                if got is None:
                    return keep[at, :]
                return keep[at, :] + got[at, :].astype(jnp.int32).astype(jnp.float32) * scale[pl.ds(c * pieces + j, 1), :]

            if pieces == 1:
                out[begin + c] = summed(0) * factor
            elif coded:
                for j in range(half):
                    to = pl.ds(pl.multiple_of(((begin + c) * half + j) * rows, rows), rows)
                    codes, power = encode(summed(half + j))
                    sent[to, :] = codes
                    powers[pl.ds((begin + c) * half + j, 1), :] = power
                    out[to, :] = summed(j)
            else:
                for j in range(pieces):
                    out[pl.ds(pl.multiple_of(((begin + c) * pieces + j) * rows, rows), rows), :] = summed(j)

        each(width, column)
        begin += width
    if coded:
        send_powers(sent, powers, begin * half * rows)


def plan_of(columns, depth):
    if depth != 4 or columns % 56 != 0:
        return [columns], [list(range(1, depth))], [[0]], [("multiply", 0)] + [("step", 0)] * (depth - 1)
    widths = [8, 10, 12, 12, 8, 6]
    paths = [[1, 3, 2, 0], [2, 1, 3, 0], [1, 3, 2], [2, 1, 3], [1, 2, 3], [1, 2, 3]]
    messages = [[2], [3], [4], [5]]
    work = [
        ("multiply", 0),
        ("multiply", 1),
        ("multiply", 2),
        ("step", 0),
        ("step", 1),
        ("multiply", 3),
        ("step", 2),
        ("multiply", 4),
        ("step", 0),
        ("multiply", 5),
        ("step", 1),
        ("step", 3),
        ("step", 2),
        ("step", 4),
        ("step", 0),
        ("step", 3),
        ("step", 0),
        ("step", 1),
        ("step", 5),
        ("step", 4),
        ("step", 3),
        ("step", 5),
        ("step", 2),
        ("step", 1),
        ("step", 4),
        ("step", 5),
    ]
    return [w * columns // 56 for w in widths], paths, messages, work


def masks_of(bits):
    masks = [0]
    for bit in reversed(bits):
        masks = masks + [m | 1 << bit for m in masks]
    return masks


def shards(owners, groups, activations, out_grad, row_blocks, doc_lengths):
    slots, features = activations.shape
    columns, entries = row_blocks.shape
    rows = entries * BLOCK // owners
    per_block = BLOCK // rows
    height = BLOCK // 2
    factor = 1.0 / float(slots * owners) ** 0.5
    widths, paths, messages, work = plan_of(columns, owners.bit_length() - 1)
    count = len(widths)
    starts = [sum(widths[:i]) for i in range(count)]

    me = lax.axis_index("dp")
    half, place = me % 2, me.astype(jnp.int32).reshape(1)

    def swap(sent, bit):
        return lax.ppermute(sent, "dp", [(o, o ^ (1 << bit)) for o in range(owners)])

    def fetch(after):
        chunks = messages[len(near_g)]
        piece = out_grad[:, starts[chunks[0]] * BLOCK : (starts[chunks[-1]] + widths[chunks[-1]]) * BLOCK]
        piece = jnp.pad(piece, ((0, PAD), (0, 0)))
        piece, after = lax.optimization_barrier((piece, after))
        near_g.append(swap(piece, 0))
        return after

    vmem = pl.BlockSpec(memory_space=pltpu.VMEM)
    smem = pl.BlockSpec(memory_space=pltpu.SMEM)
    anywhere = pl.BlockSpec(memory_space=pl.ANY)

    own, other = pl.pallas_call(
        functools.partial(prepare_kernel, rows),
        out_shape=[jax.ShapeDtypeStruct((features // 2, slots), activations.dtype)] * 2,
        in_specs=[smem, smem, vmem],
        out_specs=[vmem, vmem],
        compiler_params=params(),
        name="prepare",
    )(place, doc_lengths, activations)
    near = swap(other, 0)
    near_g = []
    own = fetch(own)
    near, near_g[0] = lax.optimization_barrier((near, near_g[0]))
    if len(messages) > 1:
        own = fetch(own)

    def spread(part):
        parts = [part] + [
            lax.ppermute(part, "mp", [(g, (g + s) % groups) for g in range(groups)]) for s in range(1, groups)
        ]
        return jnp.concatenate(parts, axis=0)

    own_t, other_t, near_t = spread(own), spread(other), spread(near)
    blocks = features // BLOCK
    picks = (lax.axis_index("mp") - row_blocks // blocks) % groups * blocks + row_blocks % blocks

    def coded(width, n):
        return jax.ShapeDtypeStruct((width * n * rows + pad16(width * n), BLOCK), jnp.int16)

    def sums(width, n):
        return jax.ShapeDtypeStruct((width * n * rows, BLOCK), jnp.float32)

    def scale(width, n):
        return pltpu.VMEM((pad16(width * n), BLOCK), jnp.float32)

    def multiply(i, last):
        width, order = widths[i], masks_of(paths[i])
        n = len(order) // 2
        begins = [starts[i]]
        if 0 in paths[i]:
            pairs, lefts, grads = ((0, 0), (1, 0)), [own_t, other_t], [out_grad]
        else:
            pairs, lefts = ((0, 0), (0, 1)), [own_t, near_t]
            at = next(m for m, chunks in enumerate(messages) if i in chunks)
            grads = [out_grad, near_g[at]]
            begins.append(starts[i] - starts[messages[at][0]])
        return pl.pallas_call(
            functools.partial(multiply_kernel, width, rows, height, order, pairs, begins),
            out_shape=[sums(width, n), coded(width, n)],
            in_specs=[smem, smem] + [vmem] * (len(lefts) + len(grads)) + [anywhere],
            out_specs=[vmem, vmem],
            scratch_shapes=[scale(width, n)],
            compiler_params=params(),
            name="multiply",
        )(place, picks[starts[i] : starts[i] + width], *lefts, *grads, last)

    def combine(sources, n, encoded, last):
        width = sum(w for w, *_ in sources)
        arrays = [a for _, *pair in sources for a in pair]
        scratch = [scale(w, n) for w, *pair in sources if len(pair) == 2]
        if n == 1:
            outs = [jax.ShapeDtypeStruct((width, rows, BLOCK), jnp.float32)]
        elif encoded:
            outs = [sums(width, n // 2), coded(width, n // 2)]
            scratch.append(scale(width, n // 2))
        else:
            outs = [sums(width, n)]
        shapes = tuple((w, len(pair) == 2) for w, *pair in sources)
        return pl.pallas_call(
            functools.partial(combine_kernel, shapes, rows, n, encoded and n > 1, factor),
            out_shape=outs,
            in_specs=[vmem] * len(arrays) + [anywhere],
            out_specs=[vmem] * len(outs),
            scratch_shapes=scratch,
            compiler_params=params(),
            name="combine",
        )(*arrays, last)

    state, outputs, last = {}, {}, place
    for what, i, *more in work:
        if what == "multiply":
            kept, sent = multiply(i, last)
            last = kept
            if len(near_g) < len(messages) and any(i == chunks[0] for chunks in messages):
                kept = fetch(kept)
            state[i] = 1, [(widths[i], kept, swap(sent, paths[i][0]))]
            continue
        if what == "send":
            step, [(width, kept, sent)] = state[i]
            sent, last = lax.optimization_barrier((sent, last))
            state[i] = step, [(width, kept, swap(sent, paths[i][step - 1]))]
            continue
        step, sources = state.pop(i)
        for j in more:
            sources = sources + state.pop(j)[1]
        width = sum(w for w, *_ in sources)
        n = 1 << (len(paths[i]) - step)
        result = combine(sources, n, what != "add", last)
        last = result[0]
        if n == 1:
            outputs[i] = result[0]
        elif what == "add":
            state[i] = step, [(width, result[0])]
        elif what == "hold":
            state[i] = step + 1, [(width, *result)]
        else:
            state[i] = step + 1, [(width, result[0], swap(result[1], paths[i][step]))]
    return jnp.concatenate([outputs[i] for i in sorted(outputs)], axis=0)


def solution(mesh):
    in_specs = (P("dp", "mp"), P("dp", "mp"), P("mp", None), P("dp", None))
    out_specs = P("mp", "dp", None)
    body = functools.partial(shards, mesh.shape["dp"], mesh.shape["mp"])
    return jax.shard_map(body, mesh=mesh, in_specs=in_specs, out_specs=out_specs, check_vma=False)
```

```python
import functools

import jax
import jax.numpy as jnp
from jax import lax
from jax.experimental import pallas as pl
from jax.experimental.pallas import tpu as pltpu
from jax.sharding import PartitionSpec as P

BLOCK = 128
LEVELS = 32700.0
STEPS = 128.0
SMALLEST = 2.0**-110
PAD = 8
VMEM_LIMIT = 16 * 1024 * 1024


def pad16(rows):
    return -(-rows // 16) * 16


def params():
    return pltpu.CompilerParams(vmem_limit_bytes=VMEM_LIMIT)


def encode(values):
    largest = jnp.max(jnp.abs(values), axis=0, keepdims=True)
    power = jnp.ceil(jnp.log2(jnp.maximum(largest, SMALLEST)) * STEPS)
    codes = jnp.round(values * (jnp.exp2(power * (-1.0 / STEPS)) * LEVELS))
    return codes.astype(jnp.int32).astype(jnp.int16), power


def send_powers(sent, powers, body):
    sent[pl.ds(body, powers.shape[0]), :] = powers[...].astype(jnp.int32).astype(jnp.int16)


def read_scales(got, scales, body):
    coded = got[pl.ds(body, scales.shape[0]), :].astype(jnp.int32).astype(jnp.float32)
    scales[...] = jnp.exp2(coded * (1.0 / STEPS)) * (1.0 / LEVELS)


def each(width, column):
    at_once = max(n for n in (1, 2, 3) if width % n == 0)

    def step(i, _):
        for j in range(at_once):
            column(i * at_once + j)
        return 0

    lax.fori_loop(0, width // at_once, step, 0)


def prepare_kernel(rows, me, lengths, activations, own, other):
    slots, features = activations.shape
    live = lengths[0, 0]
    for i in range(1, lengths.shape[1]):
        live = live + lengths[0, i]
    keep = lax.broadcasted_iota(jnp.int32, (BLOCK, slots), 1) < live
    for b in range(features // BLOCK):
        block = activations[:, b * BLOCK : (b + 1) * BLOCK].astype(jnp.float32).T
        block = jnp.where(keep, block, 0.0).astype(activations.dtype)
        for p in range(BLOCK // rows):
            to = pl.ds((b * (BLOCK // rows) + p) // 2 * rows, rows)
            piece = block[p * rows : (p + 1) * rows]

            @pl.when(me[0] % 2 == p % 2)
            def _():
                own[to, :] = piece

            @pl.when(me[0] % 2 != p % 2)
            def _():
                other[to, :] = piece


def multiply_kernel(width, rows, height, order, pairs, begins, me, picks, *refs):
    lefts, grads = refs[: len(pairs)], refs[len(pairs) : -4]
    keep, sent, powers = refs[-3:]
    half = len(order) // 2
    per_block = height // rows
    slots = lefts[0].shape[1]

    def column(c):
        lanes = [pl.ds(pl.multiple_of((begin + c) * BLOCK, BLOCK), BLOCK) for begin in begins]

        def product(masks):
            starts = []
            for mask in masks:
                piece = (me[0] ^ mask) // 2
                entry, part = piece // per_block, piece % per_block
                starts.append((mask & 1, pl.multiple_of(picks[c, entry] * height + part * rows, rows)))
            total = None
            for t, grad in enumerate(grads):
                left = [lefts[pairs.index((x, t))][pl.ds(s, rows), :] for x, s in starts]
                term = jnp.dot(
                    jnp.concatenate(left, axis=0), grad[:slots, lanes[t]], preferred_element_type=jnp.float32
                )
                total = term if total is None else total + term
            return total

        away = product(order[half:])
        for j in range(half):
            codes, power = encode(away[j * rows : (j + 1) * rows])
            sent[pl.ds(pl.multiple_of((c * half + j) * rows, rows), rows), :] = codes
            powers[pl.ds(c * half + j, 1), :] = power
        keep[pl.ds(pl.multiple_of(c * (half * rows), half * rows), half * rows), :] = product(order[:half])

    each(width, column)
    send_powers(sent, powers, width * half * rows)


def combine_kernel(sources, rows, pieces, coded, factor, *refs):
    count = sum(1 + has for _, has in sources)
    inputs, refs = list(refs[:count]), refs[count + 1 :]
    half = pieces // 2
    outs = 2 if coded else 1
    out, scales = refs[0], list(refs[outs:])
    if coded:
        sent, powers = refs[1], scales.pop()
    begin = 0
    for width, has in sources:
        keep = inputs.pop(0)
        got, scale = (inputs.pop(0), scales.pop(0)) if has else (None, None)
        if has:
            read_scales(got, scale, width * pieces * rows)

        def column(c, keep=keep, got=got, scale=scale, begin=begin):
            def summed(j):
                at = pl.ds(pl.multiple_of((c * pieces + j) * rows, rows), rows)
                if got is None:
                    return keep[at, :]
                return keep[at, :] + got[at, :].astype(jnp.int32).astype(jnp.float32) * scale[pl.ds(c * pieces + j, 1), :]

            if pieces == 1:
                out[begin + c] = summed(0) * factor
            elif coded:
                for j in range(half):
                    to = pl.ds(pl.multiple_of(((begin + c) * half + j) * rows, rows), rows)
                    codes, power = encode(summed(half + j))
                    sent[to, :] = codes
                    powers[pl.ds((begin + c) * half + j, 1), :] = power
                    out[to, :] = summed(j)
            else:
                for j in range(pieces):
                    out[pl.ds(pl.multiple_of(((begin + c) * pieces + j) * rows, rows), rows), :] = summed(j)

        each(width, column)
        begin += width
    if coded:
        send_powers(sent, powers, begin * half * rows)


def plan_of(columns, depth):
    if depth != 4 or columns % 56 != 0:
        return [columns], [list(range(1, depth))], [[0]], [("multiply", 0)] + [("step", 0)] * (depth - 1)
    widths = [8, 10, 8, 10, 10, 10]
    paths = [[1, 2, 3, 0], [2, 1, 3, 0], [1, 2, 3], [1, 2, 3], [2, 1, 3], [1, 2, 3]]
    messages = [[2], [3], [4], [5]]
    work = [
        ("multiply", 0),
        ("multiply", 1),
        ("multiply", 2),
        ("step", 0),
        ("multiply", 3),
        ("step", 1),
        ("step", 2),
        ("step", 0),
        ("multiply", 4),
        ("step", 2),
        ("step", 3),
        ("step", 0),
        ("multiply", 5),
        ("step", 4),
        ("step", 1),
        ("step", 2),
        ("step", 5),
        ("step", 3),
        ("step", 1),
        ("step", 4),
        ("step", 5),
        ("step", 0),
        ("step", 3),
        ("step", 1),
        ("step", 4),
        ("step", 5),
    ]
    return [w * columns // 56 for w in widths], paths, messages, work


def masks_of(bits):
    masks = [0]
    for bit in reversed(bits):
        masks = masks + [m | 1 << bit for m in masks]
    return masks


def shards(owners, groups, activations, out_grad, row_blocks, doc_lengths):
    slots, features = activations.shape
    columns, entries = row_blocks.shape
    rows = entries * BLOCK // owners
    per_block = BLOCK // rows
    height = BLOCK // 2
    factor = 1.0 / float(slots * owners) ** 0.5
    widths, paths, messages, work = plan_of(columns, owners.bit_length() - 1)
    count = len(widths)
    starts = [sum(widths[:i]) for i in range(count)]

    me = lax.axis_index("dp")
    half, place = me % 2, me.astype(jnp.int32).reshape(1)

    def swap(sent, bit):
        return lax.ppermute(sent, "dp", [(o, o ^ (1 << bit)) for o in range(owners)])

    def fetch(after):
        chunks = messages[len(near_g)]
        piece = out_grad[:, starts[chunks[0]] * BLOCK : (starts[chunks[-1]] + widths[chunks[-1]]) * BLOCK]
        piece = jnp.pad(piece, ((0, PAD), (0, 0)))
        piece, after = lax.optimization_barrier((piece, after))
        near_g.append(swap(piece, 0))
        return after

    vmem = pl.BlockSpec(memory_space=pltpu.VMEM)
    smem = pl.BlockSpec(memory_space=pltpu.SMEM)
    anywhere = pl.BlockSpec(memory_space=pl.ANY)

    own, other = pl.pallas_call(
        functools.partial(prepare_kernel, rows),
        out_shape=[jax.ShapeDtypeStruct((features // 2, slots), activations.dtype)] * 2,
        in_specs=[smem, smem, vmem],
        out_specs=[vmem, vmem],
        compiler_params=params(),
        name="prepare",
    )(place, doc_lengths, activations)
    near = swap(other, 0)
    near_g = []
    own = fetch(own)
    near, near_g[0] = lax.optimization_barrier((near, near_g[0]))
    if len(messages) > 1:
        own = fetch(own)

    def spread(part):
        parts = [part] + [
            lax.ppermute(part, "mp", [(g, (g + s) % groups) for g in range(groups)]) for s in range(1, groups)
        ]
        return jnp.concatenate(parts, axis=0)

    own_t, other_t, near_t = spread(own), spread(other), spread(near)
    blocks = features // BLOCK
    picks = (lax.axis_index("mp") - row_blocks // blocks) % groups * blocks + row_blocks % blocks

    def coded(width, n):
        return jax.ShapeDtypeStruct((width * n * rows + pad16(width * n), BLOCK), jnp.int16)

    def sums(width, n):
        return jax.ShapeDtypeStruct((width * n * rows, BLOCK), jnp.float32)

    def scale(width, n):
        return pltpu.VMEM((pad16(width * n), BLOCK), jnp.float32)

    def multiply(i, last):
        width, order = widths[i], masks_of(paths[i])
        n = len(order) // 2
        begins = [starts[i]]
        if 0 in paths[i]:
            pairs, lefts, grads = ((0, 0), (1, 0)), [own_t, other_t], [out_grad]
        else:
            pairs, lefts = ((0, 0), (0, 1)), [own_t, near_t]
            at = next(m for m, chunks in enumerate(messages) if i in chunks)
            grads = [out_grad, near_g[at]]
            begins.append(starts[i] - starts[messages[at][0]])
        return pl.pallas_call(
            functools.partial(multiply_kernel, width, rows, height, order, pairs, begins),
            out_shape=[sums(width, n), coded(width, n)],
            in_specs=[smem, smem] + [vmem] * (len(lefts) + len(grads)) + [anywhere],
            out_specs=[vmem, vmem],
            scratch_shapes=[scale(width, n)],
            compiler_params=params(),
            name="multiply",
        )(place, picks[starts[i] : starts[i] + width], *lefts, *grads, last)

    def combine(sources, n, encoded, last):
        width = sum(w for w, *_ in sources)
        arrays = [a for _, *pair in sources for a in pair]
        scratch = [scale(w, n) for w, *pair in sources if len(pair) == 2]
        if n == 1:
            outs = [jax.ShapeDtypeStruct((width, rows, BLOCK), jnp.float32)]
        elif encoded:
            outs = [sums(width, n // 2), coded(width, n // 2)]
            scratch.append(scale(width, n // 2))
        else:
            outs = [sums(width, n)]
        shapes = tuple((w, len(pair) == 2) for w, *pair in sources)
        return pl.pallas_call(
            functools.partial(combine_kernel, shapes, rows, n, encoded and n > 1, factor),
            out_shape=outs,
            in_specs=[vmem] * len(arrays) + [anywhere],
            out_specs=[vmem] * len(outs),
            scratch_shapes=scratch,
            compiler_params=params(),
            name="combine",
        )(*arrays, last)

    state, outputs, last = {}, {}, place
    for what, i, *more in work:
        if what == "multiply":
            kept, sent = multiply(i, last)
            last = kept
            if len(near_g) < len(messages) and any(i == chunks[0] for chunks in messages):
                kept = fetch(kept)
            state[i] = 1, [(widths[i], kept, swap(sent, paths[i][0]))]
            continue
        if what == "send":
            step, [(width, kept, sent)] = state[i]
            sent, last = lax.optimization_barrier((sent, last))
            state[i] = step, [(width, kept, swap(sent, paths[i][step - 1]))]
            continue
        step, sources = state.pop(i)
        for j in more:
            sources = sources + state.pop(j)[1]
        width = sum(w for w, *_ in sources)
        n = 1 << (len(paths[i]) - step)
        result = combine(sources, n, what != "add", last)
        last = result[0]
        if n == 1:
            outputs[i] = result[0]
        elif what == "add":
            state[i] = step, [(width, result[0])]
        elif what == "hold":
            state[i] = step + 1, [(width, *result)]
        else:
            state[i] = step + 1, [(width, result[0], swap(result[1], paths[i][step]))]
    return jnp.concatenate([outputs[i] for i in sorted(outputs)], axis=0)


def solution(mesh):
    in_specs = (P("dp", "mp"), P("dp", "mp"), P("mp", None), P("dp", None))
    out_specs = P("mp", "dp", None)
    body = functools.partial(shards, mesh.shape["dp"], mesh.shape["mp"])
    return jax.shard_map(body, mesh=mesh, in_specs=in_specs, out_specs=out_specs, check_vma=False)
```

```python
import functools

import jax
import jax.numpy as jnp
from jax import lax
from jax.experimental import pallas as pl
from jax.experimental.pallas import tpu as pltpu
from jax.sharding import PartitionSpec as P

BLOCK = 128
LEVELS = 32700.0
STEPS = 128.0
SMALLEST = 2.0**-110
PAD = 8
VMEM_LIMIT = 16 * 1024 * 1024


def pad16(rows):
    return -(-rows // 16) * 16


def params():
    return pltpu.CompilerParams(vmem_limit_bytes=VMEM_LIMIT)


def encode(values):
    largest = jnp.max(jnp.abs(values), axis=0, keepdims=True)
    power = jnp.ceil(jnp.log2(jnp.maximum(largest, SMALLEST)) * STEPS)
    codes = jnp.round(values * (jnp.exp2(power * (-1.0 / STEPS)) * LEVELS))
    return codes.astype(jnp.int32).astype(jnp.int16), power


def send_powers(sent, powers, body):
    sent[pl.ds(body, powers.shape[0]), :] = powers[...].astype(jnp.int32).astype(jnp.int16)


def read_scales(got, scales, body):
    coded = got[pl.ds(body, scales.shape[0]), :].astype(jnp.int32).astype(jnp.float32)
    scales[...] = jnp.exp2(coded * (1.0 / STEPS)) * (1.0 / LEVELS)


def each(width, column):
    at_once = max(n for n in (1, 2, 3) if width % n == 0)

    def step(i, _):
        for j in range(at_once):
            column(i * at_once + j)
        return 0

    lax.fori_loop(0, width // at_once, step, 0)


def prepare_kernel(rows, me, lengths, activations, own, other):
    slots, features = activations.shape
    live = lengths[0, 0]
    for i in range(1, lengths.shape[1]):
        live = live + lengths[0, i]
    keep = lax.broadcasted_iota(jnp.int32, (BLOCK, slots), 1) < live
    keep = jnp.where(keep, 1.0, 0.0).astype(activations.dtype)
    for b in range(features // BLOCK):
        block = activations[:, b * BLOCK : (b + 1) * BLOCK].T * keep
        for p in range(BLOCK // rows):
            to = pl.ds((b * (BLOCK // rows) + p) // 2 * rows, rows)
            piece = block[p * rows : (p + 1) * rows]

            @pl.when(me[0] % 2 == p % 2)
            def _():
                own[to, :] = piece

            @pl.when(me[0] % 2 != p % 2)
            def _():
                other[to, :] = piece


def multiply_kernel(width, rows, height, order, pairs, begins, me, picks, *refs):
    lefts, grads = refs[: len(pairs)], refs[len(pairs) : -4]
    keep, sent, powers = refs[-3:]
    half = len(order) // 2
    per_block = height // rows
    slots = lefts[0].shape[1]

    def column(c):
        lanes = [pl.ds(pl.multiple_of((begin + c) * BLOCK, BLOCK), BLOCK) for begin in begins]

        def product(masks):
            starts = []
            for mask in masks:
                piece = (me[0] ^ mask) // 2
                entry, part = piece // per_block, piece % per_block
                starts.append((mask & 1, pl.multiple_of(picks[c, entry] * height + part * rows, rows)))
            total = None
            for t, grad in enumerate(grads):
                left = [lefts[pairs.index((x, t))][pl.ds(s, rows), :] for x, s in starts]
                term = jnp.dot(
                    jnp.concatenate(left, axis=0), grad[:slots, lanes[t]], preferred_element_type=jnp.float32
                )
                total = term if total is None else total + term
            return total

        away = product(order[half:])
        for j in range(half):
            codes, power = encode(away[j * rows : (j + 1) * rows])
            sent[pl.ds(pl.multiple_of((c * half + j) * rows, rows), rows), :] = codes
            powers[pl.ds(c * half + j, 1), :] = power
        keep[pl.ds(pl.multiple_of(c * (half * rows), half * rows), half * rows), :] = product(order[:half])

    each(width, column)
    send_powers(sent, powers, width * half * rows)


def combine_kernel(sources, rows, pieces, coded, factor, *refs):
    count = sum(1 + has for _, has in sources)
    inputs, refs = list(refs[:count]), refs[count + 1 :]
    half = pieces // 2
    outs = 2 if coded else 1
    out, scales = refs[0], list(refs[outs:])
    if coded:
        sent, powers = refs[1], scales.pop()
    begin = 0
    for width, has in sources:
        keep = inputs.pop(0)
        got, scale = (inputs.pop(0), scales.pop(0)) if has else (None, None)
        if has:
            read_scales(got, scale, width * pieces * rows)

        def column(c, keep=keep, got=got, scale=scale, begin=begin):
            def summed(j):
                at = pl.ds(pl.multiple_of((c * pieces + j) * rows, rows), rows)
                if got is None:
                    return keep[at, :]
                return keep[at, :] + got[at, :].astype(jnp.int32).astype(jnp.float32) * scale[pl.ds(c * pieces + j, 1), :]

            if pieces == 1:
                out[begin + c] = summed(0) * factor
            elif coded:
                for j in range(half):
                    to = pl.ds(pl.multiple_of(((begin + c) * half + j) * rows, rows), rows)
                    codes, power = encode(summed(half + j))
                    sent[to, :] = codes
                    powers[pl.ds((begin + c) * half + j, 1), :] = power
                    out[to, :] = summed(j)
            else:
                for j in range(pieces):
                    out[pl.ds(pl.multiple_of(((begin + c) * pieces + j) * rows, rows), rows), :] = summed(j)

        each(width, column)
        begin += width
    if coded:
        send_powers(sent, powers, begin * half * rows)


def plan_of(columns, depth):
    if depth != 4 or columns % 56 != 0:
        return [columns], [list(range(1, depth))], [[0]], [("multiply", 0)] + [("step", 0)] * (depth - 1)
    widths = [8, 10, 12, 10, 10, 6]
    paths = [[2, 1, 3, 0], [1, 2, 3, 0], [2, 1, 3], [1, 2, 3], [1, 2, 3], [1, 2, 3]]
    messages = [[2], [3], [4], [5]]
    work = [
        ("multiply", 0),
        ("multiply", 1),
        ("multiply", 2),
        ("step", 0),
        ("step", 1),
        ("multiply", 3),
        ("step", 2),
        ("step", 0),
        ("multiply", 4),
        ("step", 3),
        ("multiply", 5),
        ("step", 1),
        ("step", 0),
        ("step", 4),
        ("step", 3),
        ("step", 1),
        ("step", 2),
        ("step", 3),
        ("step", 1),
        ("step", 5),
        ("step", 4),
        ("step", 2),
        ("step", 0),
        ("step", 5),
        ("step", 4),
        ("step", 5),
    ]
    return [w * columns // 56 for w in widths], paths, messages, work


def masks_of(bits):
    masks = [0]
    for bit in reversed(bits):
        masks = masks + [m | 1 << bit for m in masks]
    return masks


def shards(owners, groups, activations, out_grad, row_blocks, doc_lengths):
    slots, features = activations.shape
    columns, entries = row_blocks.shape
    rows = entries * BLOCK // owners
    per_block = BLOCK // rows
    height = BLOCK // 2
    factor = 1.0 / float(slots * owners) ** 0.5
    widths, paths, messages, work = plan_of(columns, owners.bit_length() - 1)
    count = len(widths)
    starts = [sum(widths[:i]) for i in range(count)]

    me = lax.axis_index("dp")
    half, place = me % 2, me.astype(jnp.int32).reshape(1)

    def swap(sent, bit):
        return lax.ppermute(sent, "dp", [(o, o ^ (1 << bit)) for o in range(owners)])

    def fetch(after):
        chunks = messages[len(near_g)]
        piece = out_grad[:, starts[chunks[0]] * BLOCK : (starts[chunks[-1]] + widths[chunks[-1]]) * BLOCK]
        piece = jnp.pad(piece, ((0, PAD), (0, 0)))
        piece, after = lax.optimization_barrier((piece, after))
        near_g.append(swap(piece, 0))
        return after

    vmem = pl.BlockSpec(memory_space=pltpu.VMEM)
    smem = pl.BlockSpec(memory_space=pltpu.SMEM)
    anywhere = pl.BlockSpec(memory_space=pl.ANY)

    own, other = pl.pallas_call(
        functools.partial(prepare_kernel, rows),
        out_shape=[jax.ShapeDtypeStruct((features // 2, slots), activations.dtype)] * 2,
        in_specs=[smem, smem, vmem],
        out_specs=[vmem, vmem],
        compiler_params=params(),
        name="prepare",
    )(place, doc_lengths, activations)
    near = swap(other, 0)
    near_g = []
    own = fetch(own)
    near, near_g[0] = lax.optimization_barrier((near, near_g[0]))
    if len(messages) > 1:
        own = fetch(own)

    def spread(part):
        parts = [part] + [
            lax.ppermute(part, "mp", [(g, (g + s) % groups) for g in range(groups)]) for s in range(1, groups)
        ]
        return jnp.concatenate(parts, axis=0)

    own_t, other_t, near_t = spread(own), spread(other), spread(near)
    blocks = features // BLOCK
    picks = (lax.axis_index("mp") - row_blocks // blocks) % groups * blocks + row_blocks % blocks

    def coded(width, n):
        return jax.ShapeDtypeStruct((width * n * rows + pad16(width * n), BLOCK), jnp.int16)

    def sums(width, n):
        return jax.ShapeDtypeStruct((width * n * rows, BLOCK), jnp.float32)

    def scale(width, n):
        return pltpu.VMEM((pad16(width * n), BLOCK), jnp.float32)

    def multiply(i, last):
        width, order = widths[i], masks_of(paths[i])
        n = len(order) // 2
        begins = [starts[i]]
        if 0 in paths[i]:
            pairs, lefts, grads = ((0, 0), (1, 0)), [own_t, other_t], [out_grad]
        else:
            pairs, lefts = ((0, 0), (0, 1)), [own_t, near_t]
            at = next(m for m, chunks in enumerate(messages) if i in chunks)
            grads = [out_grad, near_g[at]]
            begins.append(starts[i] - starts[messages[at][0]])
        return pl.pallas_call(
            functools.partial(multiply_kernel, width, rows, height, order, pairs, begins),
            out_shape=[sums(width, n), coded(width, n)],
            in_specs=[smem, smem] + [vmem] * (len(lefts) + len(grads)) + [anywhere],
            out_specs=[vmem, vmem],
            scratch_shapes=[scale(width, n)],
            compiler_params=params(),
            name="multiply",
        )(place, picks[starts[i] : starts[i] + width], *lefts, *grads, last)

    def combine(sources, n, encoded, last):
        width = sum(w for w, *_ in sources)
        arrays = [a for _, *pair in sources for a in pair]
        scratch = [scale(w, n) for w, *pair in sources if len(pair) == 2]
        if n == 1:
            outs = [jax.ShapeDtypeStruct((width, rows, BLOCK), jnp.float32)]
        elif encoded:
            outs = [sums(width, n // 2), coded(width, n // 2)]
            scratch.append(scale(width, n // 2))
        else:
            outs = [sums(width, n)]
        shapes = tuple((w, len(pair) == 2) for w, *pair in sources)
        return pl.pallas_call(
            functools.partial(combine_kernel, shapes, rows, n, encoded and n > 1, factor),
            out_shape=outs,
            in_specs=[vmem] * len(arrays) + [anywhere],
            out_specs=[vmem] * len(outs),
            scratch_shapes=scratch,
            compiler_params=params(),
            name="combine",
        )(*arrays, last)

    state, outputs, last = {}, {}, place
    for what, i, *more in work:
        if what == "multiply":
            kept, sent = multiply(i, last)
            last = kept
            if len(near_g) < len(messages) and any(i == chunks[0] for chunks in messages):
                kept = fetch(kept)
            state[i] = 1, [(widths[i], kept, swap(sent, paths[i][0]))]
            continue
        if what == "send":
            step, [(width, kept, sent)] = state[i]
            sent, last = lax.optimization_barrier((sent, last))
            state[i] = step, [(width, kept, swap(sent, paths[i][step - 1]))]
            continue
        step, sources = state.pop(i)
        for j in more:
            sources = sources + state.pop(j)[1]
        width = sum(w for w, *_ in sources)
        n = 1 << (len(paths[i]) - step)
        result = combine(sources, n, what != "add", last)
        last = result[0]
        if n == 1:
            outputs[i] = result[0]
        elif what == "add":
            state[i] = step, [(width, result[0])]
        elif what == "hold":
            state[i] = step + 1, [(width, *result)]
        else:
            state[i] = step + 1, [(width, result[0], swap(result[1], paths[i][step]))]
    return jnp.concatenate([outputs[i] for i in sorted(outputs)], axis=0)


def solution(mesh):
    in_specs = (P("dp", "mp"), P("dp", "mp"), P("mp", None), P("dp", None))
    out_specs = P("mp", "dp", None)
    body = functools.partial(shards, mesh.shape["dp"], mesh.shape["mp"])
    return jax.shard_map(body, mesh=mesh, in_specs=in_specs, out_specs=out_specs, check_vma=False)
```

```python
import functools

import jax
import jax.numpy as jnp
from jax import lax
from jax.experimental import pallas as pl
from jax.experimental.pallas import tpu as pltpu
from jax.sharding import PartitionSpec as P

BLOCK = 128
LEVELS = 32700.0
STEPS = 128.0
SMALLEST = 2.0**-110
PAD = 8
VMEM_LIMIT = 16 * 1024 * 1024


def pad16(rows):
    return -(-rows // 16) * 16


def params():
    return pltpu.CompilerParams(vmem_limit_bytes=VMEM_LIMIT)


def encode(values):
    largest = jnp.max(jnp.abs(values), axis=0, keepdims=True)
    power = jnp.ceil(jnp.log2(jnp.maximum(largest, SMALLEST)) * STEPS)
    codes = jnp.round(values * (jnp.exp2(power * (-1.0 / STEPS)) * LEVELS))
    return codes.astype(jnp.int32).astype(jnp.int16), power


def send_powers(sent, powers, body):
    sent[pl.ds(body, powers.shape[0]), :] = powers[...].astype(jnp.int32).astype(jnp.int16)


def read_scales(got, scales, body):
    coded = got[pl.ds(body, scales.shape[0]), :].astype(jnp.int32).astype(jnp.float32)
    scales[...] = jnp.exp2(coded * (1.0 / STEPS)) * (1.0 / LEVELS)


def each(width, column):
    at_once = max(n for n in (1, 2, 3) if width % n == 0)

    def step(i, _):
        for j in range(at_once):
            column(i * at_once + j)
        return 0

    lax.fori_loop(0, width // at_once, step, 0)


def prepare_kernel(rows, me, lengths, activations, own, other):
    slots, features = activations.shape
    live = lengths[0, 0]
    for i in range(1, lengths.shape[1]):
        live = live + lengths[0, i]
    keep = lax.broadcasted_iota(jnp.int32, (BLOCK, slots), 1) < live
    keep = jnp.where(keep, 1.0, 0.0).astype(activations.dtype)
    for b in range(features // BLOCK):
        block = activations[:, b * BLOCK : (b + 1) * BLOCK].T * keep
        for p in range(BLOCK // rows):
            to = pl.ds((b * (BLOCK // rows) + p) // 2 * rows, rows)
            piece = block[p * rows : (p + 1) * rows]

            @pl.when(me[0] % 2 == p % 2)
            def _():
                own[to, :] = piece

            @pl.when(me[0] % 2 != p % 2)
            def _():
                other[to, :] = piece


def multiply_kernel(width, rows, height, order, pairs, begins, me, picks, *refs):
    lefts, grads = refs[: len(pairs)], refs[len(pairs) : -4]
    keep, sent, powers = refs[-3:]
    half = len(order) // 2
    per_block = height // rows
    slots = lefts[0].shape[1]

    def column(c):
        lanes = [pl.ds(pl.multiple_of((begin + c) * BLOCK, BLOCK), BLOCK) for begin in begins]

        def product(masks):
            starts = []
            for mask in masks:
                piece = (me[0] ^ mask) // 2
                entry, part = piece // per_block, piece % per_block
                block = picks[begins[0] + c, entry] ^ me[1]
                starts.append((mask & 1, pl.multiple_of(block * height + part * rows, rows)))
            total = None
            for t, grad in enumerate(grads):
                left = [lefts[pairs.index((x, t))][pl.ds(s, rows), :] for x, s in starts]
                term = jnp.dot(
                    jnp.concatenate(left, axis=0), grad[:slots, lanes[t]], preferred_element_type=jnp.float32
                )
                total = term if total is None else total + term
            return total

        away = product(order[half:])
        for j in range(half):
            codes, power = encode(away[j * rows : (j + 1) * rows])
            sent[pl.ds(pl.multiple_of((c * half + j) * rows, rows), rows), :] = codes
            powers[pl.ds(c * half + j, 1), :] = power
        keep[pl.ds(pl.multiple_of(c * (half * rows), half * rows), half * rows), :] = product(order[:half])

    each(width, column)
    send_powers(sent, powers, width * half * rows)


def combine_kernel(sources, rows, pieces, coded, factor, *refs):
    count = sum(1 + has for _, has in sources)
    inputs, refs = list(refs[:count]), refs[count + 1 :]
    half = pieces // 2
    outs = 2 if coded else 1
    out, scales = refs[0], list(refs[outs:])
    if coded:
        sent, powers = refs[1], scales.pop()
    begin = 0
    for width, has in sources:
        keep = inputs.pop(0)
        got, scale = (inputs.pop(0), scales.pop(0)) if has else (None, None)
        if has:
            read_scales(got, scale, width * pieces * rows)

        def column(c, keep=keep, got=got, scale=scale, begin=begin):
            def summed(j):
                at = pl.ds(pl.multiple_of((c * pieces + j) * rows, rows), rows)
                if got is None:
                    return keep[at, :]
                return keep[at, :] + got[at, :].astype(jnp.int32).astype(jnp.float32) * scale[pl.ds(c * pieces + j, 1), :]

            if pieces == 1:
                out[begin + c] = summed(0) * factor
            elif coded:
                for j in range(half):
                    to = pl.ds(pl.multiple_of(((begin + c) * half + j) * rows, rows), rows)
                    codes, power = encode(summed(half + j))
                    sent[to, :] = codes
                    powers[pl.ds((begin + c) * half + j, 1), :] = power
                    out[to, :] = summed(j)
            else:
                for j in range(pieces):
                    out[pl.ds(pl.multiple_of(((begin + c) * pieces + j) * rows, rows), rows), :] = summed(j)

        each(width, column)
        begin += width
    if coded:
        send_powers(sent, powers, begin * half * rows)


def plan_of(columns, depth):
    if depth != 4 or columns % 56 != 0:
        return [columns], [list(range(1, depth))], [[0]], [("multiply", 0)] + [("step", 0)] * (depth - 1)
    widths = [8, 8, 14, 10, 10, 6]
    paths = [[2, 1, 3, 0], [1, 2, 3, 0], [2, 1, 3], [1, 2, 3], [1, 2, 3], [1, 2, 3]]
    messages = [[2], [3], [4], [5]]
    work = [
        ("multiply", 0),
        ("multiply", 1),
        ("multiply", 2),
        ("step", 0),
        ("multiply", 3),
        ("step", 0),
        ("step", 1),
        ("multiply", 4),
        ("step", 2),
        ("step", 3),
        ("multiply", 5),
        ("step", 1),
        ("step", 0),
        ("step", 4),
        ("step", 3),
        ("step", 1),
        ("step", 2),
        ("step", 3),
        ("step", 0),
        ("step", 5),
        ("step", 4),
        ("step", 2),
        ("step", 5),
        ("step", 1),
        ("step", 4),
        ("step", 5),
    ]
    return [w * columns // 56 for w in widths], paths, messages, work


def masks_of(bits):
    masks = [0]
    for bit in reversed(bits):
        masks = masks + [m | 1 << bit for m in masks]
    return masks


def shards(owners, groups, activations, out_grad, row_blocks, doc_lengths):
    slots, features = activations.shape
    columns, entries = row_blocks.shape
    rows = entries * BLOCK // owners
    per_block = BLOCK // rows
    height = BLOCK // 2
    factor = 1.0 / float(slots * owners) ** 0.5
    widths, paths, messages, work = plan_of(columns, owners.bit_length() - 1)
    count = len(widths)
    starts = [sum(widths[:i]) for i in range(count)]

    me = lax.axis_index("dp")
    blocks = features // BLOCK
    place = jnp.stack([me, lax.axis_index("mp") * blocks]).astype(jnp.int32)

    def swap(sent, bit):
        return lax.ppermute(sent, "dp", [(o, o ^ (1 << bit)) for o in range(owners)])

    def fetch(after):
        chunks = messages[len(near_g)]
        piece = out_grad[:, starts[chunks[0]] * BLOCK : (starts[chunks[-1]] + widths[chunks[-1]]) * BLOCK]
        piece = jnp.pad(piece, ((0, PAD), (0, 0)))
        piece, after = lax.optimization_barrier((piece, after))
        near_g.append(swap(piece, 0))
        return after

    vmem = pl.BlockSpec(memory_space=pltpu.VMEM)
    smem = pl.BlockSpec(memory_space=pltpu.SMEM)
    anywhere = pl.BlockSpec(memory_space=pl.ANY)

    own, other = pl.pallas_call(
        functools.partial(prepare_kernel, rows),
        out_shape=[jax.ShapeDtypeStruct((features // 2, slots), activations.dtype)] * 2,
        in_specs=[smem, smem, vmem],
        out_specs=[vmem, vmem],
        compiler_params=params(),
        name="prepare",
    )(place, doc_lengths, activations)
    near = swap(other, 0)
    near_g = []
    own = fetch(own)
    if len(messages) > 1:
        own = fetch(own)

    def spread(part):
        parts = [part] + [
            lax.ppermute(part, "mp", [(g, g ^ s) for g in range(groups)]) for s in range(1, groups)
        ]
        return jnp.concatenate(parts, axis=0)

    own_t, other_t, near_t = spread(own), spread(other), spread(near)

    def coded(width, n):
        return jax.ShapeDtypeStruct((width * n * rows + pad16(width * n), BLOCK), jnp.int16)

    def sums(width, n):
        return jax.ShapeDtypeStruct((width * n * rows, BLOCK), jnp.float32)

    def scale(width, n):
        return pltpu.VMEM((pad16(width * n), BLOCK), jnp.float32)

    def multiply(i, last):
        width, order = widths[i], masks_of(paths[i])
        n = len(order) // 2
        begins = [starts[i]]
        if 0 in paths[i]:
            pairs, lefts, grads = ((0, 0), (1, 0)), [own_t, other_t], [out_grad]
        else:
            pairs, lefts = ((0, 0), (0, 1)), [own_t, near_t]
            at = next(m for m, chunks in enumerate(messages) if i in chunks)
            grads = [out_grad, near_g[at]]
            begins.append(starts[i] - starts[messages[at][0]])
        return pl.pallas_call(
            functools.partial(multiply_kernel, width, rows, height, order, pairs, begins),
            out_shape=[sums(width, n), coded(width, n)],
            in_specs=[smem, smem] + [vmem] * (len(lefts) + len(grads)) + [anywhere],
            out_specs=[vmem, vmem],
            scratch_shapes=[scale(width, n)],
            compiler_params=params(),
            name="multiply",
        )(place, row_blocks, *lefts, *grads, last)

    def combine(sources, n, encoded, last):
        width = sum(w for w, *_ in sources)
        arrays = [a for _, *pair in sources for a in pair]
        scratch = [scale(w, n) for w, *pair in sources if len(pair) == 2]
        if n == 1:
            outs = [jax.ShapeDtypeStruct((width, rows, BLOCK), jnp.float32)]
        elif encoded:
            outs = [sums(width, n // 2), coded(width, n // 2)]
            scratch.append(scale(width, n // 2))
        else:
            outs = [sums(width, n)]
        shapes = tuple((w, len(pair) == 2) for w, *pair in sources)
        return pl.pallas_call(
            functools.partial(combine_kernel, shapes, rows, n, encoded and n > 1, factor),
            out_shape=outs,
            in_specs=[vmem] * len(arrays) + [anywhere],
            out_specs=[vmem] * len(outs),
            scratch_shapes=scratch,
            compiler_params=params(),
            name="combine",
        )(*arrays, last)

    state, outputs, last = {}, {}, place
    for what, i, *more in work:
        if what == "multiply":
            kept, sent = multiply(i, last)
            last = kept
            if len(near_g) < len(messages) and any(i == chunks[0] for chunks in messages):
                kept = fetch(kept)
            state[i] = 1, [(widths[i], kept, swap(sent, paths[i][0]))]
            continue
        if what == "send":
            step, [(width, kept, sent)] = state[i]
            sent, last = lax.optimization_barrier((sent, last))
            state[i] = step, [(width, kept, swap(sent, paths[i][step - 1]))]
            continue
        step, sources = state.pop(i)
        for j in more:
            sources = sources + state.pop(j)[1]
        width = sum(w for w, *_ in sources)
        n = 1 << (len(paths[i]) - step)
        result = combine(sources, n, what != "add", last)
        last = result[0]
        if n == 1:
            outputs[i] = result[0]
        elif what == "add":
            state[i] = step, [(width, result[0])]
        elif what == "hold":
            state[i] = step + 1, [(width, *result)]
        else:
            state[i] = step + 1, [(width, result[0], swap(result[1], paths[i][step]))]
    return jnp.concatenate([outputs[i] for i in sorted(outputs)], axis=0)


def solution(mesh):
    in_specs = (P("dp", "mp"), P("dp", "mp"), P("mp", None), P("dp", None))
    out_specs = P("mp", "dp", None)
    body = functools.partial(shards, mesh.shape["dp"], mesh.shape["mp"])
    return jax.shard_map(body, mesh=mesh, in_specs=in_specs, out_specs=out_specs, check_vma=False)
```

```python
import functools

import jax
import jax.numpy as jnp
from jax import lax
from jax.experimental import pallas as pl
from jax.experimental.pallas import tpu as pltpu
from jax.sharding import PartitionSpec as P

BLOCK = 128
LEVELS = 32700.0
STEPS = 128.0
SMALLEST = 2.0**-110
PAD = 8
VMEM_LIMIT = 16 * 1024 * 1024


def pad16(rows):
    return -(-rows // 16) * 16


def params():
    return pltpu.CompilerParams(vmem_limit_bytes=VMEM_LIMIT)


def encode(values):
    largest = jnp.max(jnp.abs(values), axis=0, keepdims=True)
    power = jnp.ceil(jnp.log2(jnp.maximum(largest, SMALLEST)) * STEPS)
    codes = jnp.round(values * (jnp.exp2(power * (-1.0 / STEPS)) * LEVELS))
    return codes.astype(jnp.int32).astype(jnp.int16), power


def send_powers(sent, powers, body):
    sent[pl.ds(body, powers.shape[0]), :] = powers[...].astype(jnp.int32).astype(jnp.int16)


def read_scales(got, scales, body):
    coded = got[pl.ds(body, scales.shape[0]), :].astype(jnp.int32).astype(jnp.float32)
    scales[...] = jnp.exp2(coded * (1.0 / STEPS)) * (1.0 / LEVELS)


def each(width, column):
    at_once = max(n for n in (1, 2, 3) if width % n == 0)

    def step(i, _):
        for j in range(at_once):
            column(i * at_once + j)
        return 0

    lax.fori_loop(0, width // at_once, step, 0)


def prepare_kernel(rows, me, lengths, activations, own, other):
    slots, features = activations.shape
    live = lengths[0, 0]
    for i in range(1, lengths.shape[1]):
        live = live + lengths[0, i]
    keep = lax.broadcasted_iota(jnp.int32, (BLOCK, slots), 1) < live
    keep = jnp.where(keep, 1.0, 0.0).astype(activations.dtype)
    for b in range(features // BLOCK):
        block = activations[:, b * BLOCK : (b + 1) * BLOCK].T * keep
        for p in range(BLOCK // rows):
            to = pl.ds((b * (BLOCK // rows) + p) // 2 * rows, rows)
            piece = block[p * rows : (p + 1) * rows]

            @pl.when(me[0] % 2 == p % 2)
            def _():
                own[to, :] = piece

            @pl.when(me[0] % 2 != p % 2)
            def _():
                other[to, :] = piece


def multiply_kernel(width, rows, height, order, pairs, begins, me, picks, *refs):
    lefts, grads = refs[: len(pairs)], refs[len(pairs) : -4]
    keep, sent, powers = refs[-3:]
    half = len(order) // 2
    per_block = height // rows
    slots = lefts[0].shape[1]

    def column(c):
        lanes = [pl.ds(pl.multiple_of((begin + c) * BLOCK, BLOCK), BLOCK) for begin in begins]

        def product(masks):
            starts = []
            for mask in masks:
                piece = (me[0] ^ mask) // 2
                entry, part = piece // per_block, piece % per_block
                block = picks[c, entry] ^ me[1]
                starts.append((mask & 1, pl.multiple_of(block * height + part * rows, rows)))
            total = None
            for t, grad in enumerate(grads):
                left = [lefts[pairs.index((x, t))][pl.ds(s, rows), :] for x, s in starts]
                term = jnp.dot(
                    jnp.concatenate(left, axis=0), grad[:slots, lanes[t]], preferred_element_type=jnp.float32
                )
                total = term if total is None else total + term
            return total

        away = product(order[half:])
        for j in range(half):
            codes, power = encode(away[j * rows : (j + 1) * rows])
            sent[pl.ds(pl.multiple_of((c * half + j) * rows, rows), rows), :] = codes
            powers[pl.ds(c * half + j, 1), :] = power
        keep[pl.ds(pl.multiple_of(c * (half * rows), half * rows), half * rows), :] = product(order[:half])

    each(width, column)
    send_powers(sent, powers, width * half * rows)


def combine_kernel(sources, rows, pieces, coded, factor, *refs):
    count = sum(1 + has for _, has in sources)
    inputs, refs = list(refs[:count]), refs[count + 1 :]
    half = pieces // 2
    outs = 2 if coded else 1
    out, scales = refs[0], list(refs[outs:])
    if coded:
        sent, powers = refs[1], scales.pop()
    begin = 0
    for width, has in sources:
        keep = inputs.pop(0)
        got, scale = (inputs.pop(0), scales.pop(0)) if has else (None, None)
        if has:
            read_scales(got, scale, width * pieces * rows)

        def column(c, keep=keep, got=got, scale=scale, begin=begin):
            def summed(j):
                at = pl.ds(pl.multiple_of((c * pieces + j) * rows, rows), rows)
                if got is None:
                    return keep[at, :]
                return keep[at, :] + got[at, :].astype(jnp.int32).astype(jnp.float32) * scale[pl.ds(c * pieces + j, 1), :]

            if pieces == 1:
                out[begin + c] = summed(0) * factor
            elif coded:
                for j in range(half):
                    to = pl.ds(pl.multiple_of(((begin + c) * half + j) * rows, rows), rows)
                    codes, power = encode(summed(half + j))
                    sent[to, :] = codes
                    powers[pl.ds((begin + c) * half + j, 1), :] = power
                    out[to, :] = summed(j)
            else:
                for j in range(pieces):
                    out[pl.ds(pl.multiple_of(((begin + c) * pieces + j) * rows, rows), rows), :] = summed(j)

        each(width, column)
        begin += width
    if coded:
        send_powers(sent, powers, begin * half * rows)


def plan_of(columns, depth):
    if depth != 4 or columns % 56 != 0:
        return [columns], [list(range(1, depth))], [[0]], [("multiply", 0)] + [("step", 0)] * (depth - 1)
    widths = [8, 8, 14, 10, 10, 6]
    paths = [[2, 1, 3, 0], [1, 2, 3, 0], [2, 1, 3], [1, 2, 3], [1, 2, 3], [1, 2, 3]]
    messages = [[2], [3], [4], [5]]
    work = [
        ("multiply", 0),
        ("multiply", 1),
        ("multiply", 2),
        ("step", 0),
        ("multiply", 3),
        ("step", 0),
        ("step", 1),
        ("multiply", 4),
        ("step", 2),
        ("step", 3),
        ("multiply", 5),
        ("step", 1),
        ("step", 0),
        ("step", 4),
        ("step", 3),
        ("step", 1),
        ("step", 2),
        ("step", 3),
        ("step", 0),
        ("step", 5),
        ("step", 4),
        ("step", 2),
        ("step", 5),
        ("step", 1),
        ("step", 4),
        ("step", 5),
    ]
    return [w * columns // 56 for w in widths], paths, messages, work


def masks_of(bits):
    masks = [0]
    for bit in reversed(bits):
        masks = masks + [m | 1 << bit for m in masks]
    return masks


def shards(owners, groups, activations, out_grad, row_blocks, doc_lengths):
    slots, features = activations.shape
    columns, entries = row_blocks.shape
    rows = entries * BLOCK // owners
    per_block = BLOCK // rows
    height = BLOCK // 2
    factor = 1.0 / float(slots * owners) ** 0.5
    widths, paths, messages, work = plan_of(columns, owners.bit_length() - 1)
    count = len(widths)
    starts = [sum(widths[:i]) for i in range(count)]

    me = lax.axis_index("dp")
    blocks = features // BLOCK
    place = jnp.stack([me, lax.axis_index("mp") * blocks]).astype(jnp.int32)

    def swap(sent, bit):
        return lax.ppermute(sent, "dp", [(o, o ^ (1 << bit)) for o in range(owners)])

    def fetch(after):
        chunks = messages[len(near_g)]
        whole, after = lax.optimization_barrier((out_grad, after))
        piece = whole[:, starts[chunks[0]] * BLOCK : (starts[chunks[-1]] + widths[chunks[-1]]) * BLOCK]
        piece = jnp.pad(piece, ((0, PAD), (0, 0)))
        near_g.append(swap(piece, 0))
        return after

    vmem = pl.BlockSpec(memory_space=pltpu.VMEM)
    smem = pl.BlockSpec(memory_space=pltpu.SMEM)
    anywhere = pl.BlockSpec(memory_space=pl.ANY)

    own, other = pl.pallas_call(
        functools.partial(prepare_kernel, rows),
        out_shape=[jax.ShapeDtypeStruct((features // 2, slots), activations.dtype)] * 2,
        in_specs=[smem, smem, vmem],
        out_specs=[vmem, vmem],
        compiler_params=params(),
        name="prepare",
    )(place, doc_lengths, activations)
    near = swap(other, 0)
    near_g = []
    own = fetch(own)
    if len(messages) > 1:
        own = fetch(own)

    def spread(part):
        parts = [part] + [
            lax.ppermute(part, "mp", [(g, g ^ s) for g in range(groups)]) for s in range(1, groups)
        ]
        return jnp.concatenate(parts, axis=0)

    own_t, other_t = spread(own), spread(other)
    near_t = []

    def coded(width, n):
        return jax.ShapeDtypeStruct((width * n * rows + pad16(width * n), BLOCK), jnp.int16)

    def sums(width, n):
        return jax.ShapeDtypeStruct((width * n * rows, BLOCK), jnp.float32)

    def scale(width, n):
        return pltpu.VMEM((pad16(width * n), BLOCK), jnp.float32)

    def multiply(i, last):
        width, order = widths[i], masks_of(paths[i])
        n = len(order) // 2
        begins = [starts[i]]
        if 0 in paths[i]:
            pairs, lefts, grads = ((0, 0), (1, 0)), [own_t, other_t], [out_grad]
        else:
            pairs, lefts = ((0, 0), (0, 1)), [own_t, near_t[0]]
            at = next(m for m, chunks in enumerate(messages) if i in chunks)
            grads = [out_grad, near_g[at]]
            begins.append(starts[i] - starts[messages[at][0]])
        return pl.pallas_call(
            functools.partial(multiply_kernel, width, rows, height, order, pairs, begins),
            out_shape=[sums(width, n), coded(width, n)],
            in_specs=[smem, smem] + [vmem] * (len(lefts) + len(grads)) + [anywhere],
            out_specs=[vmem, vmem],
            scratch_shapes=[scale(width, n)],
            compiler_params=params(),
            name="multiply",
        )(place, row_blocks[starts[i] : starts[i] + width], *lefts, *grads, last)

    def combine(sources, n, encoded, last):
        width = sum(w for w, *_ in sources)
        arrays = [a for _, *pair in sources for a in pair]
        scratch = [scale(w, n) for w, *pair in sources if len(pair) == 2]
        if n == 1:
            outs = [jax.ShapeDtypeStruct((width, rows, BLOCK), jnp.float32)]
        elif encoded:
            outs = [sums(width, n // 2), coded(width, n // 2)]
            scratch.append(scale(width, n // 2))
        else:
            outs = [sums(width, n)]
        shapes = tuple((w, len(pair) == 2) for w, *pair in sources)
        return pl.pallas_call(
            functools.partial(combine_kernel, shapes, rows, n, encoded and n > 1, factor),
            out_shape=outs,
            in_specs=[vmem] * len(arrays) + [anywhere],
            out_specs=[vmem] * len(outs),
            scratch_shapes=scratch,
            compiler_params=params(),
            name="combine",
        )(*arrays, last)

    state, outputs, last = {}, {}, place
    for what, i, *more in work:
        if what == "multiply":
            if not near_t and 0 not in paths[i]:
                if state:
                    j = max(state)
                    step, [(width, kept, *rest)] = state[j]
                    near, kept = lax.optimization_barrier((near, kept))
                    state[j] = step, [(width, kept, *rest)]
                near_t.append(spread(near))
            kept, sent = multiply(i, last)
            last = kept
            if len(near_g) < len(messages) and any(i == chunks[0] for chunks in messages):
                kept = fetch(kept)
            state[i] = 1, [(widths[i], kept, swap(sent, paths[i][0]))]
            continue
        if what == "send":
            step, [(width, kept, sent)] = state[i]
            sent, last = lax.optimization_barrier((sent, last))
            state[i] = step, [(width, kept, swap(sent, paths[i][step - 1]))]
            continue
        step, sources = state.pop(i)
        for j in more:
            sources = sources + state.pop(j)[1]
        width = sum(w for w, *_ in sources)
        n = 1 << (len(paths[i]) - step)
        result = combine(sources, n, what != "add", last)
        last = result[0]
        if n == 1:
            outputs[i] = result[0]
        elif what == "add":
            state[i] = step, [(width, result[0])]
        elif what == "hold":
            state[i] = step + 1, [(width, *result)]
        else:
            state[i] = step + 1, [(width, result[0], swap(result[1], paths[i][step]))]
    return jnp.concatenate([outputs[i] for i in sorted(outputs)], axis=0)


def solution(mesh):
    in_specs = (P("dp", "mp"), P("dp", "mp"), P("mp", None), P("dp", None))
    out_specs = P("mp", "dp", None)
    body = functools.partial(shards, mesh.shape["dp"], mesh.shape["mp"])
    return jax.shard_map(body, mesh=mesh, in_specs=in_specs, out_specs=out_specs, check_vma=False)
```

```python
import functools

import jax
import jax.numpy as jnp
from jax import lax
from jax.experimental import pallas as pl
from jax.experimental.pallas import tpu as pltpu
from jax.sharding import PartitionSpec as P

BLOCK = 128
LEVELS = 32700.0
STEPS = 128.0
SMALLEST = 2.0**-110
PAD = 8
VMEM_LIMIT = 16 * 1024 * 1024


def pad16(rows):
    return -(-rows // 16) * 16


def params():
    return pltpu.CompilerParams(vmem_limit_bytes=VMEM_LIMIT)


def encode(values):
    largest = jnp.max(jnp.abs(values), axis=0, keepdims=True)
    power = jnp.ceil(jnp.log2(jnp.maximum(largest, SMALLEST)) * STEPS)
    codes = jnp.round(values * (jnp.exp2(power * (-1.0 / STEPS)) * LEVELS))
    return codes.astype(jnp.int32).astype(jnp.int16), power


def send_powers(sent, powers, body):
    sent[pl.ds(body, powers.shape[0]), :] = powers[...].astype(jnp.int32).astype(jnp.int16)


def read_scales(got, scales, body):
    coded = got[pl.ds(body, scales.shape[0]), :].astype(jnp.int32).astype(jnp.float32)
    scales[...] = jnp.exp2(coded * (1.0 / STEPS)) * (1.0 / LEVELS)


def each(width, column):
    at_once = max(n for n in (1, 2, 3) if width % n == 0)

    def step(i, _):
        for j in range(at_once):
            column(i * at_once + j)
        return 0

    lax.fori_loop(0, width // at_once, step, 0)


def prepare_kernel(rows, me, lengths, activations, own, other):
    slots, features = activations.shape
    live = lengths[0, 0]
    for i in range(1, lengths.shape[1]):
        live = live + lengths[0, i]
    keep = lax.broadcasted_iota(jnp.int32, (BLOCK, slots), 1) < live
    keep = jnp.where(keep, 1.0, 0.0).astype(activations.dtype)
    for b in range(features // BLOCK):
        block = activations[:, b * BLOCK : (b + 1) * BLOCK].T * keep
        for p in range(BLOCK // rows):
            to = pl.ds((b * (BLOCK // rows) + p) // 2 * rows, rows)
            piece = block[p * rows : (p + 1) * rows]

            @pl.when(me[0] % 2 == p % 2)
            def _():
                own[to, :] = piece

            @pl.when(me[0] % 2 != p % 2)
            def _():
                other[to, :] = piece


def multiply_kernel(width, rows, height, order, pairs, begins, me, picks, *refs):
    lefts, grads = refs[: len(pairs)], refs[len(pairs) : -4]
    keep, sent, powers = refs[-3:]
    half = len(order) // 2
    per_block = height // rows
    slots = lefts[0].shape[1]

    def column(c):
        lanes = [pl.ds(pl.multiple_of((begin + c) * BLOCK, BLOCK), BLOCK) for begin in begins]

        def product(masks):
            starts = []
            for mask in masks:
                piece = (me[0] ^ mask) // 2
                entry, part = piece // per_block, piece % per_block
                block = picks[begins[0] + c, entry] ^ me[1]
                starts.append((mask & 1, pl.multiple_of(block * height + part * rows, rows)))
            total = None
            for t, grad in enumerate(grads):
                left = [lefts[pairs.index((x, t))][pl.ds(s, rows), :] for x, s in starts]
                term = jnp.dot(
                    jnp.concatenate(left, axis=0), grad[:slots, lanes[t]], preferred_element_type=jnp.float32
                )
                total = term if total is None else total + term
            return total

        away = product(order[half:])
        for j in range(half):
            codes, power = encode(away[j * rows : (j + 1) * rows])
            sent[pl.ds(pl.multiple_of((c * half + j) * rows, rows), rows), :] = codes
            powers[pl.ds(c * half + j, 1), :] = power
        keep[pl.ds(pl.multiple_of(c * (half * rows), half * rows), half * rows), :] = product(order[:half])

    each(width, column)
    send_powers(sent, powers, width * half * rows)


def combine_kernel(sources, rows, pieces, coded, factor, *refs):
    count = sum(1 + has for _, has in sources)
    inputs, refs = list(refs[:count]), refs[count + 1 :]
    half = pieces // 2
    outs = 2 if coded else 1
    out, scales = refs[0], list(refs[outs:])
    if coded:
        sent, powers = refs[1], scales.pop()
    begin = 0
    for width, has in sources:
        keep = inputs.pop(0)
        got, scale = (inputs.pop(0), scales.pop(0)) if has else (None, None)
        if has:
            read_scales(got, scale, width * pieces * rows)

        def column(c, keep=keep, got=got, scale=scale, begin=begin):
            def summed(j):
                at = pl.ds(pl.multiple_of((c * pieces + j) * rows, rows), rows)
                if got is None:
                    return keep[at, :]
                return keep[at, :] + got[at, :].astype(jnp.int32).astype(jnp.float32) * scale[pl.ds(c * pieces + j, 1), :]

            if pieces == 1:
                out[begin + c] = summed(0) * factor
            elif coded:
                for j in range(half):
                    to = pl.ds(pl.multiple_of(((begin + c) * half + j) * rows, rows), rows)
                    codes, power = encode(summed(half + j))
                    sent[to, :] = codes
                    powers[pl.ds((begin + c) * half + j, 1), :] = power
                    out[to, :] = summed(j)
            else:
                for j in range(pieces):
                    out[pl.ds(pl.multiple_of(((begin + c) * pieces + j) * rows, rows), rows), :] = summed(j)

        each(width, column)
        begin += width
    if coded:
        send_powers(sent, powers, begin * half * rows)


def plan_of(columns, depth):
    if depth != 4 or columns % 56 != 0:
        return [columns], [list(range(1, depth))], [[0]], [("multiply", 0)] + [("step", 0)] * (depth - 1)
    widths = [8, 8, 14, 10, 10, 6]
    paths = [[2, 1, 3, 0], [1, 2, 3, 0], [2, 1, 3], [1, 2, 3], [1, 2, 3], [1, 2, 3]]
    messages = [[2], [3], [4], [5]]
    work = [
        ("multiply", 0),
        ("multiply", 1),
        ("multiply", 2),
        ("step", 0),
        ("multiply", 3),
        ("step", 0),
        ("step", 1),
        ("multiply", 4),
        ("step", 2),
        ("step", 3),
        ("multiply", 5),
        ("step", 1),
        ("step", 0),
        ("step", 4),
        ("step", 3),
        ("step", 1),
        ("step", 2),
        ("step", 3),
        ("step", 0),
        ("step", 5),
        ("step", 4),
        ("step", 2),
        ("step", 5),
        ("step", 1),
        ("step", 4),
        ("step", 5),
    ]
    return [w * columns // 56 for w in widths], paths, messages, work


def masks_of(bits):
    masks = [0]
    for bit in reversed(bits):
        masks = masks + [m | 1 << bit for m in masks]
    return masks


def shards(owners, groups, activations, out_grad, row_blocks, doc_lengths):
    slots, features = activations.shape
    columns, entries = row_blocks.shape
    rows = entries * BLOCK // owners
    per_block = BLOCK // rows
    height = BLOCK // 2
    factor = 1.0 / float(slots * owners) ** 0.5
    widths, paths, messages, work = plan_of(columns, owners.bit_length() - 1)
    count = len(widths)
    starts = [sum(widths[:i]) for i in range(count)]

    me = lax.axis_index("dp")
    blocks = features // BLOCK
    place = jnp.stack([me, lax.axis_index("mp") * blocks]).astype(jnp.int32)

    def swap(sent, bit):
        return lax.ppermute(sent, "dp", [(o, o ^ (1 << bit)) for o in range(owners)])

    def fetch(after):
        chunks = messages[len(near_g)]
        piece = out_grad[:, starts[chunks[0]] * BLOCK : (starts[chunks[-1]] + widths[chunks[-1]]) * BLOCK]
        piece = jnp.pad(piece, ((0, PAD), (0, 0)))
        piece, after = lax.optimization_barrier((piece, after))
        near_g.append(swap(piece, 0))
        return after

    vmem = pl.BlockSpec(memory_space=pltpu.VMEM)
    smem = pl.BlockSpec(memory_space=pltpu.SMEM)
    anywhere = pl.BlockSpec(memory_space=pl.ANY)

    own, other = pl.pallas_call(
        functools.partial(prepare_kernel, rows),
        out_shape=[jax.ShapeDtypeStruct((features // 2, slots), activations.dtype)] * 2,
        in_specs=[smem, smem, vmem],
        out_specs=[vmem, vmem],
        compiler_params=params(),
        name="prepare",
    )(place, doc_lengths, activations)
    near = swap(other, 0)
    near_g = []
    own = fetch(own)
    if len(messages) > 1:
        own = fetch(own)

    def spread(part):
        parts = [part] + [
            lax.ppermute(part, "mp", [(g, g ^ s) for g in range(groups)]) for s in range(1, groups)
        ]
        return jnp.concatenate(parts, axis=0)

    own_t, other_t = spread(own), spread(other)
    near_t = []

    def coded(width, n):
        return jax.ShapeDtypeStruct((width * n * rows + pad16(width * n), BLOCK), jnp.int16)

    def sums(width, n):
        return jax.ShapeDtypeStruct((width * n * rows, BLOCK), jnp.float32)

    def scale(width, n):
        return pltpu.VMEM((pad16(width * n), BLOCK), jnp.float32)

    def multiply(i, last):
        width, order = widths[i], masks_of(paths[i])
        n = len(order) // 2
        begins = [starts[i]]
        if 0 in paths[i]:
            pairs, lefts, grads = ((0, 0), (1, 0)), [own_t, other_t], [out_grad]
        else:
            pairs, lefts = ((0, 0), (0, 1)), [own_t, near_t[0]]
            at = next(m for m, chunks in enumerate(messages) if i in chunks)
            grads = [out_grad, near_g[at]]
            begins.append(starts[i] - starts[messages[at][0]])
        return pl.pallas_call(
            functools.partial(multiply_kernel, width, rows, height, order, pairs, begins),
            out_shape=[sums(width, n), coded(width, n)],
            in_specs=[smem, smem] + [vmem] * (len(lefts) + len(grads)) + [anywhere],
            out_specs=[vmem, vmem],
            scratch_shapes=[scale(width, n)],
            compiler_params=params(),
            name="multiply",
        )(place, row_blocks, *lefts, *grads, last)

    def combine(sources, n, encoded, last):
        width = sum(w for w, *_ in sources)
        arrays = [a for _, *pair in sources for a in pair]
        scratch = [scale(w, n) for w, *pair in sources if len(pair) == 2]
        if n == 1:
            outs = [jax.ShapeDtypeStruct((width, rows, BLOCK), jnp.float32)]
        elif encoded:
            outs = [sums(width, n // 2), coded(width, n // 2)]
            scratch.append(scale(width, n // 2))
        else:
            outs = [sums(width, n)]
        shapes = tuple((w, len(pair) == 2) for w, *pair in sources)
        return pl.pallas_call(
            functools.partial(combine_kernel, shapes, rows, n, encoded and n > 1, factor),
            out_shape=outs,
            in_specs=[vmem] * len(arrays) + [anywhere],
            out_specs=[vmem] * len(outs),
            scratch_shapes=scratch,
            compiler_params=params(),
            name="combine",
        )(*arrays, last)

    state, outputs, last = {}, {}, place
    for what, i, *more in work:
        if what == "multiply":
            if not near_t and 0 not in paths[i]:
                if state:
                    j = max(state)
                    step, [(width, kept, *rest)] = state[j]
                    near, kept = lax.optimization_barrier((near, kept))
                    state[j] = step, [(width, kept, *rest)]
                near_t.append(spread(near))
            kept, sent = multiply(i, last)
            last = kept
            if len(near_g) < len(messages) and any(i == chunks[0] for chunks in messages):
                kept = fetch(kept)
            state[i] = 1, [(widths[i], kept, swap(sent, paths[i][0]))]
            continue
        if what == "send":
            step, [(width, kept, sent)] = state[i]
            sent, last = lax.optimization_barrier((sent, last))
            state[i] = step, [(width, kept, swap(sent, paths[i][step - 1]))]
            continue
        step, sources = state.pop(i)
        for j in more:
            sources = sources + state.pop(j)[1]
        width = sum(w for w, *_ in sources)
        n = 1 << (len(paths[i]) - step)
        result = combine(sources, n, what != "add", last)
        last = result[0]
        if n == 1:
            outputs[i] = result[0]
        elif what == "add":
            state[i] = step, [(width, result[0])]
        elif what == "hold":
            state[i] = step + 1, [(width, *result)]
        else:
            state[i] = step + 1, [(width, result[0], swap(result[1], paths[i][step]))]
    return jnp.concatenate([outputs[i] for i in sorted(outputs)], axis=0)


def solution(mesh):
    in_specs = (P("dp", "mp"), P("dp", "mp"), P("mp", None), P("dp", None))
    out_specs = P("mp", "dp", None)
    body = functools.partial(shards, mesh.shape["dp"], mesh.shape["mp"])
    return jax.shard_map(body, mesh=mesh, in_specs=in_specs, out_specs=out_specs, check_vma=False)
```

```python
import functools

import jax
import jax.numpy as jnp
from jax import lax
from jax.experimental import pallas as pl
from jax.experimental.pallas import tpu as pltpu
from jax.sharding import PartitionSpec as P

BLOCK = 128
LEVELS = 32700.0
STEPS = 128.0
SMALLEST = 2.0**-110
PAD = 8
VMEM_LIMIT = 16 * 1024 * 1024


def pad16(rows):
    return -(-rows // 16) * 16


def params():
    return pltpu.CompilerParams(vmem_limit_bytes=VMEM_LIMIT)


def encode(values):
    largest = jnp.max(jnp.abs(values), axis=0, keepdims=True)
    power = jnp.ceil(jnp.log2(jnp.maximum(largest, SMALLEST)) * STEPS)
    codes = jnp.round(values * (jnp.exp2(power * (-1.0 / STEPS)) * LEVELS))
    return codes.astype(jnp.int32).astype(jnp.int16), power


def send_powers(sent, powers, body):
    sent[pl.ds(body, powers.shape[0]), :] = powers[...].astype(jnp.int32).astype(jnp.int16)


def read_scales(got, scales, body):
    coded = got[pl.ds(body, scales.shape[0]), :].astype(jnp.int32).astype(jnp.float32)
    scales[...] = jnp.exp2(coded * (1.0 / STEPS)) * (1.0 / LEVELS)


def each(width, column):
    at_once = max(n for n in (1, 2, 3) if width % n == 0)

    def step(i, _):
        for j in range(at_once):
            column(i * at_once + j)
        return 0

    lax.fori_loop(0, width // at_once, step, 0)


def prepare_kernel(rows, me, lengths, activations, own, other):
    slots, features = activations.shape
    live = lengths[0, 0]
    for i in range(1, lengths.shape[1]):
        live = live + lengths[0, i]
    keep = lax.broadcasted_iota(jnp.int32, (BLOCK, slots), 1) < live
    keep = jnp.where(keep, 1.0, 0.0).astype(activations.dtype)
    for b in range(features // BLOCK):
        block = activations[:, b * BLOCK : (b + 1) * BLOCK].T * keep
        for p in range(BLOCK // rows):
            to = pl.ds((b * (BLOCK // rows) + p) // 2 * rows, rows)
            piece = block[p * rows : (p + 1) * rows]

            @pl.when(me[0] % 2 == p % 2)
            def _():
                own[to, :] = piece

            @pl.when(me[0] % 2 != p % 2)
            def _():
                other[to, :] = piece


def multiply_kernel(width, rows, height, order, pairs, begins, me, picks, *refs):
    lefts, grads = refs[: len(pairs)], refs[len(pairs) : -4]
    keep, sent, powers = refs[-3:]
    half = len(order) // 2
    per_block = height // rows
    slots = lefts[0].shape[1]

    def column(c):
        lanes = [pl.ds(pl.multiple_of((begin + c) * BLOCK, BLOCK), BLOCK) for begin in begins]

        def product(masks):
            starts = []
            for mask in masks:
                piece = (me[0] ^ mask) // 2
                entry, part = piece // per_block, piece % per_block
                block = picks[begins[0] + c, entry] ^ me[1]
                starts.append((mask & 1, pl.multiple_of(block * height + part * rows, rows)))
            total = None
            for t, grad in enumerate(grads):
                left = [lefts[pairs.index((x, t))][pl.ds(s, rows), :] for x, s in starts]
                term = jnp.dot(
                    jnp.concatenate(left, axis=0), grad[:slots, lanes[t]], preferred_element_type=jnp.float32
                )
                total = term if total is None else total + term
            return total

        away = product(order[half:])
        for j in range(half):
            codes, power = encode(away[j * rows : (j + 1) * rows])
            sent[pl.ds(pl.multiple_of((c * half + j) * rows, rows), rows), :] = codes
            powers[pl.ds(c * half + j, 1), :] = power
        keep[pl.ds(pl.multiple_of(c * (half * rows), half * rows), half * rows), :] = product(order[:half])

    each(width, column)
    send_powers(sent, powers, width * half * rows)


def combine_kernel(sources, rows, pieces, coded, factor, *refs):
    count = sum(1 + has for _, has in sources)
    inputs, refs = list(refs[:count]), refs[count + 1 :]
    half = pieces // 2
    outs = 2 if coded else 1
    out, scales = refs[0], list(refs[outs:])
    if coded:
        sent, powers = refs[1], scales.pop()
    begin = 0
    for width, has in sources:
        keep = inputs.pop(0)
        got, scale = (inputs.pop(0), scales.pop(0)) if has else (None, None)
        if has:
            read_scales(got, scale, width * pieces * rows)

        def column(c, keep=keep, got=got, scale=scale, begin=begin):
            def summed(j):
                at = pl.ds(pl.multiple_of((c * pieces + j) * rows, rows), rows)
                if got is None:
                    return keep[at, :]
                return keep[at, :] + got[at, :].astype(jnp.int32).astype(jnp.float32) * scale[pl.ds(c * pieces + j, 1), :]

            if pieces == 1:
                out[begin + c] = summed(0) * factor
            elif coded:
                for j in range(half):
                    to = pl.ds(pl.multiple_of(((begin + c) * half + j) * rows, rows), rows)
                    codes, power = encode(summed(half + j))
                    sent[to, :] = codes
                    powers[pl.ds((begin + c) * half + j, 1), :] = power
                    out[to, :] = summed(j)
            else:
                for j in range(pieces):
                    out[pl.ds(pl.multiple_of(((begin + c) * pieces + j) * rows, rows), rows), :] = summed(j)

        each(width, column)
        begin += width
    if coded:
        send_powers(sent, powers, begin * half * rows)


def plan_of(columns, depth):
    if depth != 4 or columns % 56 != 0:
        return [columns], [list(range(1, depth))], [[0]], [("multiply", 0)] + [("step", 0)] * (depth - 1)
    widths = [8, 8, 10, 10, 10, 10]
    paths = [[1, 2, 3, 0], [2, 1, 3, 0], [1, 2, 3], [1, 2, 3], [2, 1, 3], [1, 2, 3]]
    messages = [[2], [3], [4], [5]]
    work = [
        ("multiply", 0),
        ("multiply", 1),
        ("multiply", 2),
        ("step", 0),
        ("multiply", 3),
        ("step", 1),
        ("step", 2),
        ("step", 0),
        ("multiply", 4),
        ("step", 1),
        ("step", 0),
        ("step", 2),
        ("multiply", 5),
        ("step", 3),
        ("step", 4),
        ("step", 2),
        ("step", 5),
        ("step", 3),
        ("step", 1),
        ("step", 4),
        ("step", 1),
        ("step", 3),
        ("step", 5),
        ("step", 0),
        ("step", 4),
        ("step", 5),
    ]
    return [w * columns // 56 for w in widths], paths, messages, work


def masks_of(bits):
    masks = [0]
    for bit in reversed(bits):
        masks = masks + [m | 1 << bit for m in masks]
    return masks


def shards(owners, groups, activations, out_grad, row_blocks, doc_lengths):
    slots, features = activations.shape
    columns, entries = row_blocks.shape
    rows = entries * BLOCK // owners
    per_block = BLOCK // rows
    height = BLOCK // 2
    factor = 1.0 / float(slots * owners) ** 0.5
    widths, paths, messages, work = plan_of(columns, owners.bit_length() - 1)
    count = len(widths)
    starts = [sum(widths[:i]) for i in range(count)]

    me = lax.axis_index("dp")
    blocks = features // BLOCK
    place = jnp.stack([me, lax.axis_index("mp") * blocks]).astype(jnp.int32)

    def swap(sent, bit):
        return lax.ppermute(sent, "dp", [(o, o ^ (1 << bit)) for o in range(owners)])

    def fetch(after):
        chunks = messages[len(near_g)]
        piece = out_grad[:, starts[chunks[0]] * BLOCK : (starts[chunks[-1]] + widths[chunks[-1]]) * BLOCK]
        piece = jnp.pad(piece, ((0, PAD), (0, 0)))
        piece, after = lax.optimization_barrier((piece, after))
        near_g.append(swap(piece, 0))
        return after

    vmem = pl.BlockSpec(memory_space=pltpu.VMEM)
    smem = pl.BlockSpec(memory_space=pltpu.SMEM)
    anywhere = pl.BlockSpec(memory_space=pl.ANY)

    own, other = pl.pallas_call(
        functools.partial(prepare_kernel, rows),
        out_shape=[jax.ShapeDtypeStruct((features // 2, slots), activations.dtype)] * 2,
        in_specs=[smem, smem, vmem],
        out_specs=[vmem, vmem],
        compiler_params=params(),
        name="prepare",
    )(place, doc_lengths, activations)
    near = swap(other, 0)
    near_g = []
    own = fetch(own)
    if len(messages) > 1:
        own = fetch(own)

    def spread(part):
        parts = [part] + [
            lax.ppermute(part, "mp", [(g, g ^ s) for g in range(groups)]) for s in range(1, groups)
        ]
        return jnp.concatenate(parts, axis=0)

    own_t, other_t, near_t = spread(own), spread(other), spread(near)

    def coded(width, n):
        return jax.ShapeDtypeStruct((width * n * rows + pad16(width * n), BLOCK), jnp.int16)

    def sums(width, n):
        return jax.ShapeDtypeStruct((width * n * rows, BLOCK), jnp.float32)

    def scale(width, n):
        return pltpu.VMEM((pad16(width * n), BLOCK), jnp.float32)

    def multiply(i, last):
        width, order = widths[i], masks_of(paths[i])
        n = len(order) // 2
        begins = [starts[i]]
        if 0 in paths[i]:
            pairs, lefts, grads = ((0, 0), (1, 0)), [own_t, other_t], [out_grad]
        else:
            pairs, lefts = ((0, 0), (0, 1)), [own_t, near_t]
            at = next(m for m, chunks in enumerate(messages) if i in chunks)
            grads = [out_grad, near_g[at]]
            begins.append(starts[i] - starts[messages[at][0]])
        return pl.pallas_call(
            functools.partial(multiply_kernel, width, rows, height, order, pairs, begins),
            out_shape=[sums(width, n), coded(width, n)],
            in_specs=[smem, smem] + [vmem] * (len(lefts) + len(grads)) + [anywhere],
            out_specs=[vmem, vmem],
            scratch_shapes=[scale(width, n)],
            compiler_params=params(),
            name="multiply",
        )(place, row_blocks, *lefts, *grads, last)

    def combine(sources, n, encoded, last):
        width = sum(w for w, *_ in sources)
        arrays = [a for _, *pair in sources for a in pair]
        scratch = [scale(w, n) for w, *pair in sources if len(pair) == 2]
        if n == 1:
            outs = [jax.ShapeDtypeStruct((width, rows, BLOCK), jnp.float32)]
        elif encoded:
            outs = [sums(width, n // 2), coded(width, n // 2)]
            scratch.append(scale(width, n // 2))
        else:
            outs = [sums(width, n)]
        shapes = tuple((w, len(pair) == 2) for w, *pair in sources)
        return pl.pallas_call(
            functools.partial(combine_kernel, shapes, rows, n, encoded and n > 1, factor),
            out_shape=outs,
            in_specs=[vmem] * len(arrays) + [anywhere],
            out_specs=[vmem] * len(outs),
            scratch_shapes=scratch,
            compiler_params=params(),
            name="combine",
        )(*arrays, last)

    state, outputs, last = {}, {}, place
    for what, i, *more in work:
        if what == "multiply":
            kept, sent = multiply(i, last)
            last = kept
            if len(near_g) < len(messages) and any(i == chunks[0] for chunks in messages):
                kept = fetch(kept)
            state[i] = 1, [(widths[i], kept, swap(sent, paths[i][0]))]
            continue
        if what == "send":
            step, [(width, kept, sent)] = state[i]
            sent, last = lax.optimization_barrier((sent, last))
            state[i] = step, [(width, kept, swap(sent, paths[i][step - 1]))]
            continue
        step, sources = state.pop(i)
        for j in more:
            sources = sources + state.pop(j)[1]
        width = sum(w for w, *_ in sources)
        n = 1 << (len(paths[i]) - step)
        result = combine(sources, n, what != "add", last)
        last = result[0]
        if n == 1:
            outputs[i] = result[0]
        elif what == "add":
            state[i] = step, [(width, result[0])]
        elif what == "hold":
            state[i] = step + 1, [(width, *result)]
        else:
            state[i] = step + 1, [(width, result[0], swap(result[1], paths[i][step]))]
    return jnp.concatenate([outputs[i] for i in sorted(outputs)], axis=0)


def solution(mesh):
    in_specs = (P("dp", "mp"), P("dp", "mp"), P("mp", None), P("dp", None))
    out_specs = P("mp", "dp", None)
    body = functools.partial(shards, mesh.shape["dp"], mesh.shape["mp"])
    return jax.shard_map(body, mesh=mesh, in_specs=in_specs, out_specs=out_specs, check_vma=False)
```

```python
import functools

import jax
import jax.numpy as jnp
from jax import lax
from jax.experimental import pallas as pl
from jax.experimental.pallas import tpu as pltpu
from jax.sharding import PartitionSpec as P

BLOCK = 128
LEVELS = 32700.0
STEPS = 128.0
SMALLEST = 2.0**-110
PAD = 8
VMEM_LIMIT = 16 * 1024 * 1024


def pad16(rows):
    return -(-rows // 16) * 16


def params():
    return pltpu.CompilerParams(vmem_limit_bytes=VMEM_LIMIT)


def encode(values):
    largest = jnp.max(jnp.abs(values), axis=0, keepdims=True)
    power = jnp.ceil(jnp.log2(jnp.maximum(largest, SMALLEST)) * STEPS)
    codes = jnp.round(values * (jnp.exp2(power * (-1.0 / STEPS)) * LEVELS))
    return codes.astype(jnp.int32).astype(jnp.int16), power


def send_powers(sent, powers, body):
    sent[pl.ds(body, powers.shape[0]), :] = powers[...].astype(jnp.int32).astype(jnp.int16)


def read_scales(got, scales, body):
    coded = got[pl.ds(body, scales.shape[0]), :].astype(jnp.int32).astype(jnp.float32)
    scales[...] = jnp.exp2(coded * (1.0 / STEPS)) * (1.0 / LEVELS)


def each(width, column):
    at_once = max(n for n in (1, 2, 3) if width % n == 0)

    def step(i, _):
        for j in range(at_once):
            column(i * at_once + j)
        return 0

    lax.fori_loop(0, width // at_once, step, 0)


def prepare_kernel(rows, me, lengths, activations, own, other):
    slots, features = activations.shape
    live = lengths[0, 0]
    for i in range(1, lengths.shape[1]):
        live = live + lengths[0, i]
    keep = lax.broadcasted_iota(jnp.int32, (BLOCK, slots), 1) < live
    keep = jnp.where(keep, 1.0, 0.0).astype(activations.dtype)
    for b in range(features // BLOCK):
        block = activations[:, b * BLOCK : (b + 1) * BLOCK].T * keep
        for p in range(BLOCK // rows):
            to = pl.ds((b * (BLOCK // rows) + p) // 2 * rows, rows)
            piece = block[p * rows : (p + 1) * rows]

            @pl.when(me[0] % 2 == p % 2)
            def _():
                own[to, :] = piece

            @pl.when(me[0] % 2 != p % 2)
            def _():
                other[to, :] = piece


def multiply_kernel(width, rows, height, order, pairs, begins, me, picks, *refs):
    lefts, grads = refs[: len(pairs)], refs[len(pairs) : -4]
    keep, sent, powers = refs[-3:]
    half = len(order) // 2
    per_block = height // rows
    slots = lefts[0].shape[1]

    def column(c):
        lanes = [pl.ds(pl.multiple_of((begin + c) * BLOCK, BLOCK), BLOCK) for begin in begins]

        def product(masks):
            starts = []
            for mask in masks:
                piece = (me[0] ^ mask) // 2
                entry, part = piece // per_block, piece % per_block
                block = picks[c, entry] ^ me[1]
                starts.append((mask & 1, pl.multiple_of(block * height + part * rows, rows)))
            total = None
            for t, grad in enumerate(grads):
                left = [lefts[pairs.index((x, t))][pl.ds(s, rows), :] for x, s in starts]
                term = jnp.dot(
                    jnp.concatenate(left, axis=0), grad[:slots, lanes[t]], preferred_element_type=jnp.float32
                )
                total = term if total is None else total + term
            return total

        away = product(order[half:])
        for j in range(half):
            codes, power = encode(away[j * rows : (j + 1) * rows])
            sent[pl.ds(pl.multiple_of((c * half + j) * rows, rows), rows), :] = codes
            powers[pl.ds(c * half + j, 1), :] = power
        keep[pl.ds(pl.multiple_of(c * (half * rows), half * rows), half * rows), :] = product(order[:half])

    each(width, column)
    send_powers(sent, powers, width * half * rows)


def combine_kernel(sources, rows, pieces, coded, factor, *refs):
    count = sum(1 + has for _, has in sources)
    inputs, refs = list(refs[:count]), refs[count + 1 :]
    half = pieces // 2
    outs = 2 if coded else 1
    out, scales = refs[0], list(refs[outs:])
    if coded:
        sent, powers = refs[1], scales.pop()
    begin = 0
    for width, has in sources:
        keep = inputs.pop(0)
        got, scale = (inputs.pop(0), scales.pop(0)) if has else (None, None)
        if has:
            read_scales(got, scale, width * pieces * rows)

        def column(c, keep=keep, got=got, scale=scale, begin=begin):
            def summed(j):
                at = pl.ds(pl.multiple_of((c * pieces + j) * rows, rows), rows)
                if got is None:
                    return keep[at, :]
                return keep[at, :] + got[at, :].astype(jnp.int32).astype(jnp.float32) * scale[pl.ds(c * pieces + j, 1), :]

            if pieces == 1:
                out[begin + c] = summed(0) * factor
            elif coded:
                for j in range(half):
                    to = pl.ds(pl.multiple_of(((begin + c) * half + j) * rows, rows), rows)
                    codes, power = encode(summed(half + j))
                    sent[to, :] = codes
                    powers[pl.ds((begin + c) * half + j, 1), :] = power
                    out[to, :] = summed(j)
            else:
                for j in range(pieces):
                    out[pl.ds(pl.multiple_of(((begin + c) * pieces + j) * rows, rows), rows), :] = summed(j)

        each(width, column)
        begin += width
    if coded:
        send_powers(sent, powers, begin * half * rows)


def plan_of(columns, depth):
    if depth != 4 or columns % 56 != 0:
        return [columns], [list(range(1, depth))], [[0]], [("multiply", 0)] + [("step", 0)] * (depth - 1)
    widths = [8, 8, 14, 10, 10, 6]
    paths = [[2, 1, 3, 0], [1, 2, 3, 0], [2, 1, 3], [1, 2, 3], [1, 2, 3], [1, 2, 3]]
    messages = [[2], [3], [4], [5]]
    work = [
        ("multiply", 0),
        ("multiply", 1),
        ("multiply", 2),
        ("step", 0),
        ("multiply", 3),
        ("step", 0),
        ("step", 1),
        ("multiply", 4),
        ("step", 2),
        ("step", 3),
        ("multiply", 5),
        ("step", 1),
        ("step", 0),
        ("step", 4),
        ("step", 3),
        ("step", 1),
        ("step", 2),
        ("step", 3),
        ("step", 0),
        ("step", 5),
        ("step", 4),
        ("step", 2),
        ("step", 5),
        ("step", 1),
        ("step", 4),
        ("step", 5),
    ]
    return [w * columns // 56 for w in widths], paths, messages, work


def masks_of(bits):
    masks = [0]
    for bit in reversed(bits):
        masks = masks + [m | 1 << bit for m in masks]
    return masks


def shards(owners, groups, activations, out_grad, row_blocks, doc_lengths):
    slots, features = activations.shape
    columns, entries = row_blocks.shape
    rows = entries * BLOCK // owners
    per_block = BLOCK // rows
    height = BLOCK // 2
    factor = 1.0 / float(slots * owners) ** 0.5
    widths, paths, messages, work = plan_of(columns, owners.bit_length() - 1)
    count = len(widths)
    starts = [sum(widths[:i]) for i in range(count)]

    me = lax.axis_index("dp")
    blocks = features // BLOCK
    place = jnp.stack([me, lax.axis_index("mp") * blocks]).astype(jnp.int32)

    def swap(sent, bit):
        return lax.ppermute(sent, "dp", [(o, o ^ (1 << bit)) for o in range(owners)])

    def fetch(after):
        chunks = messages[len(near_g)]
        piece = out_grad[:, starts[chunks[0]] * BLOCK : (starts[chunks[-1]] + widths[chunks[-1]]) * BLOCK]
        piece = jnp.pad(piece, ((0, PAD), (0, 0)))
        piece, after = lax.optimization_barrier((piece, after))
        near_g.append(swap(piece, 0))
        return after

    vmem = pl.BlockSpec(memory_space=pltpu.VMEM)
    smem = pl.BlockSpec(memory_space=pltpu.SMEM)
    anywhere = pl.BlockSpec(memory_space=pl.ANY)

    own, other = pl.pallas_call(
        functools.partial(prepare_kernel, rows),
        out_shape=[jax.ShapeDtypeStruct((features // 2, slots), activations.dtype)] * 2,
        in_specs=[smem, smem, vmem],
        out_specs=[vmem, vmem],
        compiler_params=params(),
        name="prepare",
    )(place, doc_lengths, activations)
    near = swap(other, 0)
    near_g = []
    own = fetch(own)
    if len(messages) > 1:
        own = fetch(own)

    def spread(part):
        parts = [part] + [
            lax.ppermute(part, "mp", [(g, g ^ s) for g in range(groups)]) for s in range(1, groups)
        ]
        return jnp.concatenate(parts, axis=0)

    own_t, other_t, near_t = spread(own), spread(other), spread(near)

    def coded(width, n):
        return jax.ShapeDtypeStruct((width * n * rows + pad16(width * n), BLOCK), jnp.int16)

    def sums(width, n):
        return jax.ShapeDtypeStruct((width * n * rows, BLOCK), jnp.float32)

    def scale(width, n):
        return pltpu.VMEM((pad16(width * n), BLOCK), jnp.float32)

    def multiply(i, last):
        width, order = widths[i], masks_of(paths[i])
        n = len(order) // 2
        begins = [starts[i]]
        if 0 in paths[i]:
            pairs, lefts, grads = ((0, 0), (1, 0)), [own_t, other_t], [out_grad]
        else:
            pairs, lefts = ((0, 0), (0, 1)), [own_t, near_t]
            at = next(m for m, chunks in enumerate(messages) if i in chunks)
            grads = [out_grad, near_g[at]]
            begins.append(starts[i] - starts[messages[at][0]])
        return pl.pallas_call(
            functools.partial(multiply_kernel, width, rows, height, order, pairs, begins),
            out_shape=[sums(width, n), coded(width, n)],
            in_specs=[smem, smem] + [vmem] * (len(lefts) + len(grads)) + [anywhere],
            out_specs=[vmem, vmem],
            scratch_shapes=[scale(width, n)],
            compiler_params=params(),
            name="multiply",
        )(place, row_blocks[starts[i] : starts[i] + width], *lefts, *grads, last)

    def combine(sources, n, encoded, last):
        width = sum(w for w, *_ in sources)
        arrays = [a for _, *pair in sources for a in pair]
        scratch = [scale(w, n) for w, *pair in sources if len(pair) == 2]
        if n == 1:
            outs = [jax.ShapeDtypeStruct((width, rows, BLOCK), jnp.float32)]
        elif encoded:
            outs = [sums(width, n // 2), coded(width, n // 2)]
            scratch.append(scale(width, n // 2))
        else:
            outs = [sums(width, n)]
        shapes = tuple((w, len(pair) == 2) for w, *pair in sources)
        return pl.pallas_call(
            functools.partial(combine_kernel, shapes, rows, n, encoded and n > 1, factor),
            out_shape=outs,
            in_specs=[vmem] * len(arrays) + [anywhere],
            out_specs=[vmem] * len(outs),
            scratch_shapes=scratch,
            compiler_params=params(),
            name="combine",
        )(*arrays, last)

    state, outputs, last = {}, {}, place
    for what, i, *more in work:
        if what == "multiply":
            kept, sent = multiply(i, last)
            last = kept
            if len(near_g) < len(messages) and any(i == chunks[0] for chunks in messages):
                kept = fetch(kept)
            state[i] = 1, [(widths[i], kept, swap(sent, paths[i][0]))]
            continue
        if what == "send":
            step, [(width, kept, sent)] = state[i]
            sent, last = lax.optimization_barrier((sent, last))
            state[i] = step, [(width, kept, swap(sent, paths[i][step - 1]))]
            continue
        step, sources = state.pop(i)
        for j in more:
            sources = sources + state.pop(j)[1]
        width = sum(w for w, *_ in sources)
        n = 1 << (len(paths[i]) - step)
        result = combine(sources, n, what != "add", last)
        last = result[0]
        if n == 1:
            outputs[i] = result[0]
        elif what == "add":
            state[i] = step, [(width, result[0])]
        elif what == "hold":
            state[i] = step + 1, [(width, *result)]
        else:
            state[i] = step + 1, [(width, result[0], swap(result[1], paths[i][step]))]
    return jnp.concatenate([outputs[i] for i in sorted(outputs)], axis=0)


def solution(mesh):
    in_specs = (P("dp", "mp"), P("dp", "mp"), P("mp", None), P("dp", None))
    out_specs = P("mp", "dp", None)
    body = functools.partial(shards, mesh.shape["dp"], mesh.shape["mp"])
    return jax.shard_map(body, mesh=mesh, in_specs=in_specs, out_specs=out_specs, check_vma=False)
```

```python
import functools

import jax
import jax.numpy as jnp
from jax import lax
from jax.experimental import pallas as pl
from jax.experimental.pallas import tpu as pltpu
from jax.sharding import PartitionSpec as P

BLOCK = 128
LEVELS = 32700.0
STEPS = 128.0
SMALLEST = 2.0**-110
PAD = 8
VMEM_LIMIT = 16 * 1024 * 1024


def pad16(rows):
    return -(-rows // 16) * 16


def params():
    return pltpu.CompilerParams(vmem_limit_bytes=VMEM_LIMIT)


def encode(values):
    largest = jnp.max(jnp.abs(values), axis=0, keepdims=True)
    power = jnp.ceil(jnp.log2(jnp.maximum(largest, SMALLEST)) * STEPS)
    codes = jnp.round(values * (jnp.exp2(power * (-1.0 / STEPS)) * LEVELS))
    return codes.astype(jnp.int32).astype(jnp.int16), power


def send_powers(sent, powers, body):
    sent[pl.ds(body, powers.shape[0]), :] = powers[...].astype(jnp.int32).astype(jnp.int16)


def read_scales(got, scales, body):
    coded = got[pl.ds(body, scales.shape[0]), :].astype(jnp.int32).astype(jnp.float32)
    scales[...] = jnp.exp2(coded * (1.0 / STEPS)) * (1.0 / LEVELS)


def each(width, column):
    at_once = max(n for n in (1, 2, 3) if width % n == 0)

    def step(i, _):
        for j in range(at_once):
            column(i * at_once + j)
        return 0

    lax.fori_loop(0, width // at_once, step, 0)


def prepare_kernel(rows, me, lengths, activations, own, other):
    slots, features = activations.shape
    live = lengths[0, 0]
    for i in range(1, lengths.shape[1]):
        live = live + lengths[0, i]
    keep = lax.broadcasted_iota(jnp.int32, (BLOCK, slots), 1) < live
    keep = jnp.where(keep, 1.0, 0.0).astype(activations.dtype)
    for b in range(features // BLOCK):
        block = activations[:, b * BLOCK : (b + 1) * BLOCK].T * keep
        for p in range(BLOCK // rows):
            to = pl.ds((b * (BLOCK // rows) + p) // 2 * rows, rows)
            piece = block[p * rows : (p + 1) * rows]

            @pl.when(me[0] % 2 == p % 2)
            def _():
                own[to, :] = piece

            @pl.when(me[0] % 2 != p % 2)
            def _():
                other[to, :] = piece


def multiply_kernel(width, rows, height, order, pairs, begins, me, picks, *refs):
    lefts, grads = refs[: len(pairs)], refs[len(pairs) : -4]
    keep, sent, powers = refs[-3:]
    half = len(order) // 2
    per_block = height // rows
    slots = lefts[0].shape[1]

    def column(c):
        lanes = [pl.ds(pl.multiple_of((begin + c) * BLOCK, BLOCK), BLOCK) for begin in begins]

        def product(masks):
            starts = []
            for mask in masks:
                piece = (me[0] ^ mask) // 2
                entry, part = piece // per_block, piece % per_block
                block = picks[begins[0] + c, entry] ^ me[1]
                starts.append((mask & 1, pl.multiple_of(block * height + part * rows, rows)))
            total = None
            for t, grad in enumerate(grads):
                left = [lefts[pairs.index((x, t))][pl.ds(s, rows), :] for x, s in starts]
                term = jnp.dot(
                    jnp.concatenate(left, axis=0), grad[:slots, lanes[t]], preferred_element_type=jnp.float32
                )
                total = term if total is None else total + term
            return total

        away = product(order[half:])
        for j in range(half):
            codes, power = encode(away[j * rows : (j + 1) * rows])
            sent[pl.ds(pl.multiple_of((c * half + j) * rows, rows), rows), :] = codes
            powers[pl.ds(c * half + j, 1), :] = power
        keep[pl.ds(pl.multiple_of(c * (half * rows), half * rows), half * rows), :] = product(order[:half])

    each(width, column)
    send_powers(sent, powers, width * half * rows)


def combine_kernel(sources, rows, pieces, coded, factor, *refs):
    count = sum(1 + has for _, has in sources)
    inputs, refs = list(refs[:count]), refs[count + 1 :]
    half = pieces // 2
    outs = 2 if coded else 1
    out, scales = refs[0], list(refs[outs:])
    if coded:
        sent, powers = refs[1], scales.pop()
    begin = 0
    for width, has in sources:
        keep = inputs.pop(0)
        got, scale = (inputs.pop(0), scales.pop(0)) if has else (None, None)
        if has:
            read_scales(got, scale, width * pieces * rows)

        def column(c, keep=keep, got=got, scale=scale, begin=begin):
            def summed(j):
                at = pl.ds(pl.multiple_of((c * pieces + j) * rows, rows), rows)
                if got is None:
                    return keep[at, :]
                return keep[at, :] + got[at, :].astype(jnp.int32).astype(jnp.float32) * scale[pl.ds(c * pieces + j, 1), :]

            if pieces == 1:
                out[begin + c] = summed(0) * factor
            elif coded:
                for j in range(half):
                    to = pl.ds(pl.multiple_of(((begin + c) * half + j) * rows, rows), rows)
                    codes, power = encode(summed(half + j))
                    sent[to, :] = codes
                    powers[pl.ds((begin + c) * half + j, 1), :] = power
                    out[to, :] = summed(j)
            else:
                for j in range(pieces):
                    out[pl.ds(pl.multiple_of(((begin + c) * pieces + j) * rows, rows), rows), :] = summed(j)

        each(width, column)
        begin += width
    if coded:
        send_powers(sent, powers, begin * half * rows)


def plan_of(columns, depth):
    if depth != 4 or columns % 56 != 0:
        return [columns], [list(range(1, depth))], [[0]], [("multiply", 0)] + [("step", 0)] * (depth - 1)
    widths = [8, 8, 14, 10, 10, 6]
    paths = [[2, 1, 3, 0], [1, 2, 3, 0], [2, 1, 3], [1, 2, 3], [1, 2, 3], [1, 2, 3]]
    messages = [[2], [3], [4], [5]]
    work = [
        ("multiply", 0),
        ("multiply", 1),
        ("multiply", 2),
        ("step", 0),
        ("multiply", 3),
        ("step", 0),
        ("step", 1),
        ("multiply", 4),
        ("step", 2),
        ("step", 3),
        ("multiply", 5),
        ("step", 1),
        ("step", 0),
        ("step", 4),
        ("step", 3),
        ("step", 1),
        ("step", 2),
        ("step", 3),
        ("step", 0),
        ("step", 5),
        ("step", 4),
        ("step", 2),
        ("step", 5),
        ("step", 1),
        ("step", 4),
        ("step", 5),
    ]
    return [w * columns // 56 for w in widths], paths, messages, work


def masks_of(bits):
    masks = [0]
    for bit in reversed(bits):
        masks = masks + [m | 1 << bit for m in masks]
    return masks


def shards(owners, groups, activations, out_grad, row_blocks, doc_lengths):
    slots, features = activations.shape
    columns, entries = row_blocks.shape
    rows = entries * BLOCK // owners
    per_block = BLOCK // rows
    height = BLOCK // 2
    factor = 1.0 / float(slots * owners) ** 0.5
    widths, paths, messages, work = plan_of(columns, owners.bit_length() - 1)
    count = len(widths)
    starts = [sum(widths[:i]) for i in range(count)]

    me = lax.axis_index("dp")
    blocks = features // BLOCK
    place = jnp.stack([me, lax.axis_index("mp") * blocks]).astype(jnp.int32)

    def swap(sent, bit):
        return lax.ppermute(sent, "dp", [(o, o ^ (1 << bit)) for o in range(owners)])

    def fetch(after):
        chunks = messages[len(near_g)]
        whole, after = lax.optimization_barrier((out_grad, after))
        piece = whole[:, starts[chunks[0]] * BLOCK : (starts[chunks[-1]] + widths[chunks[-1]]) * BLOCK]
        piece = jnp.pad(piece, ((0, PAD), (0, 0)))
        near_g.append(swap(piece, 0))
        return after

    vmem = pl.BlockSpec(memory_space=pltpu.VMEM)
    smem = pl.BlockSpec(memory_space=pltpu.SMEM)
    anywhere = pl.BlockSpec(memory_space=pl.ANY)

    own, other = pl.pallas_call(
        functools.partial(prepare_kernel, rows),
        out_shape=[jax.ShapeDtypeStruct((features // 2, slots), activations.dtype)] * 2,
        in_specs=[smem, smem, vmem],
        out_specs=[vmem, vmem],
        compiler_params=params(),
        name="prepare",
    )(place, doc_lengths, activations)
    near = swap(other, 0)
    near_g = []
    own = fetch(own)
    if len(messages) > 1:
        own = fetch(own)

    def spread(part):
        parts = [part] + [
            lax.ppermute(part, "mp", [(g, g ^ s) for g in range(groups)]) for s in range(1, groups)
        ]
        return jnp.concatenate(parts, axis=0)

    own_t, other_t, near_t = spread(own), spread(other), spread(near)

    def coded(width, n):
        return jax.ShapeDtypeStruct((width * n * rows + pad16(width * n), BLOCK), jnp.int16)

    def sums(width, n):
        return jax.ShapeDtypeStruct((width * n * rows, BLOCK), jnp.float32)

    def scale(width, n):
        return pltpu.VMEM((pad16(width * n), BLOCK), jnp.float32)

    def multiply(i, last):
        width, order = widths[i], masks_of(paths[i])
        n = len(order) // 2
        begins = [starts[i]]
        if 0 in paths[i]:
            pairs, lefts, grads = ((0, 0), (1, 0)), [own_t, other_t], [out_grad]
        else:
            pairs, lefts = ((0, 0), (0, 1)), [own_t, near_t]
            at = next(m for m, chunks in enumerate(messages) if i in chunks)
            grads = [out_grad, near_g[at]]
            begins.append(starts[i] - starts[messages[at][0]])
        return pl.pallas_call(
            functools.partial(multiply_kernel, width, rows, height, order, pairs, begins),
            out_shape=[sums(width, n), coded(width, n)],
            in_specs=[smem, smem] + [vmem] * (len(lefts) + len(grads)) + [anywhere],
            out_specs=[vmem, vmem],
            scratch_shapes=[scale(width, n)],
            compiler_params=params(),
            name="multiply",
        )(place, row_blocks, *lefts, *grads, last)

    def combine(sources, n, encoded, last):
        width = sum(w for w, *_ in sources)
        arrays = [a for _, *pair in sources for a in pair]
        scratch = [scale(w, n) for w, *pair in sources if len(pair) == 2]
        if n == 1:
            outs = [jax.ShapeDtypeStruct((width, rows, BLOCK), jnp.float32)]
        elif encoded:
            outs = [sums(width, n // 2), coded(width, n // 2)]
            scratch.append(scale(width, n // 2))
        else:
            outs = [sums(width, n)]
        shapes = tuple((w, len(pair) == 2) for w, *pair in sources)
        return pl.pallas_call(
            functools.partial(combine_kernel, shapes, rows, n, encoded and n > 1, factor),
            out_shape=outs,
            in_specs=[vmem] * len(arrays) + [anywhere],
            out_specs=[vmem] * len(outs),
            scratch_shapes=scratch,
            compiler_params=params(),
            name="combine",
        )(*arrays, last)

    state, outputs, last = {}, {}, place
    for what, i, *more in work:
        if what == "multiply":
            kept, sent = multiply(i, last)
            last = kept
            if len(near_g) < len(messages) and any(i == chunks[0] for chunks in messages):
                kept = fetch(kept)
            state[i] = 1, [(widths[i], kept, swap(sent, paths[i][0]))]
            continue
        if what == "send":
            step, [(width, kept, sent)] = state[i]
            sent, last = lax.optimization_barrier((sent, last))
            state[i] = step, [(width, kept, swap(sent, paths[i][step - 1]))]
            continue
        step, sources = state.pop(i)
        for j in more:
            sources = sources + state.pop(j)[1]
        width = sum(w for w, *_ in sources)
        n = 1 << (len(paths[i]) - step)
        result = combine(sources, n, what != "add", last)
        last = result[0]
        if n == 1:
            outputs[i] = result[0]
        elif what == "add":
            state[i] = step, [(width, result[0])]
        elif what == "hold":
            state[i] = step + 1, [(width, *result)]
        else:
            state[i] = step + 1, [(width, result[0], swap(result[1], paths[i][step]))]
    return jnp.concatenate([outputs[i] for i in sorted(outputs)], axis=0)


def solution(mesh):
    in_specs = (P("dp", "mp"), P("dp", "mp"), P("mp", None), P("dp", None))
    out_specs = P("mp", "dp", None)
    body = functools.partial(shards, mesh.shape["dp"], mesh.shape["mp"])
    return jax.shard_map(body, mesh=mesh, in_specs=in_specs, out_specs=out_specs, check_vma=False)
```
